512 devices in a mesh: group: 16 (over z_hi, x, core), blk: 32 (over z_lo, y).
Axes of the slice: x: 4, y: 8, z: 8 (z_hi: 2, z_lo: 4; z = z_hi * 4 + z_lo), core: 2. Of those that a mesh axis runs over, the one named last changes fastest.
Arguments:
- teacher: bfloat16 [65536, 1024], P(('group', 'blk')), may hold values from -300 to 300
- student: bfloat16 [65536, 768], P(('group', 'blk')), may hold values from -300 to 300
Outputs:
- student_grad: float32 [65536, 768], P(('group', 'blk'))
- mean_loss: float32 [], replicated
The draws below stay inside these ranges and needn't reach their ends.
All inputs are finite; a program needn't handle non-finite values.
Results may differ from the reference program's by a relative error of at most 0.039.
Values may be sent and summed in bfloat16 or wider, within the bound.
A program may use at most 64 MiB of HBM per device.

```python
import math
import jax
import jax.numpy as jnp
from jax import lax

DT = 1024
DS = 768
BATCH = 4096
TOTAL = 65536
N_GROUP = 16


def factor_noise(key, shape):
    normal_part = jax.random.truncated_normal(jax.random.fold_in(key, 1), -3.5, 3.5, shape, jnp.float32)
    return normal_part


def speaker_layout(key):
    batch_index = jnp.arange(TOTAL) // BATCH
    speaker_count = max(BATCH // 64, 2)
    accents = jax.random.randint(jax.random.fold_in(key, 31), (TOTAL,), 0, 4) + batch_index * 4
    speakers = jax.random.randint(jax.random.fold_in(key, 32), (TOTAL,), 0, speaker_count) + batch_index * speaker_count
    return (accents, speakers, speaker_count)


def row_scales(key, top_scale):
    position = jnp.arange(TOTAL).astype(jnp.float32) / TOTAL
    spread = jnp.exp(jax.random.uniform(key, (TOTAL,), jnp.float32) * math.log(top_scale))
    return 3.0 ** position * spread


def utterance_latent(key, accents, speakers, speaker_count, width):
    batches = TOTAL // BATCH
    accent_table = 0.8 * factor_noise(jax.random.fold_in(key, 41), (batches * 4, width))
    speaker_table = 0.5 * factor_noise(jax.random.fold_in(key, 42), (batches * speaker_count, width))
    utterance = 0.5 * factor_noise(jax.random.fold_in(key, 43), (TOTAL, width))
    return accent_table[accents] + speaker_table[speakers] + utterance


def teacher_parts(key, top_scale):
    accents, speakers, speaker_count = speaker_layout(key)
    scales = row_scales(jax.random.fold_in(key, 51), top_scale)
    latent = utterance_latent(jax.random.fold_in(key, 52), accents, speakers, speaker_count, DT)
    return (scales, accents, speakers, speaker_count, latent)


def draw_teacher(key, part):
    scales, accents, speakers, speaker_count, latent = teacher_parts(key, 10.0)
    return (latent * scales[:, None]).astype(jnp.bfloat16)


def draw_student(key, part):
    scales, accents, speakers, speaker_count, latent = teacher_parts(key, 10.0)
    key = jax.random.fold_in(key, 2)
    own_scales = row_scales(jax.random.fold_in(key, 53), 10.0)
    own = utterance_latent(jax.random.fold_in(key, 61), accents, speakers, speaker_count, DS)
    values = 0.8 * latent[:, :DS] + 0.6 * own
    return (values * own_scales[:, None]).astype(jnp.bfloat16)


def setup_inputs(seed: int = 0) -> dict:
    streams_of = jax.random.split(jax.random.key(seed), 3)
    return {
        "teacher": draw_teacher(jax.random.fold_in(streams_of[2], 71), 0),
        "student": draw_student(jax.random.fold_in(streams_of[2], 71), 0),
    }


def pair_distances(embedded):
    squares = lax.optimization_barrier(jnp.sum(jnp.square(embedded.astype(jnp.float32)), 1))
    products = jnp.dot(embedded, embedded.T, preferred_element_type=jnp.float32)
    spread = squares[:, None] + squares[None, :] - 2.0 * products
    return jnp.sqrt(jnp.maximum(spread, 0.0) + 1.0)

def reference(teacher, student):
    teacher_groups = teacher.reshape(N_GROUP, BATCH, DT)
    student_groups = student.reshape(N_GROUP, BATCH, DS)
    off_diagonal = jnp.logical_not(jnp.eye(BATCH, dtype=bool))
    pair_count = 1.0 * N_GROUP * BATCH * (BATCH - 1)

    def first_pass(blocks):
        dist_teacher = pair_distances(blocks[0])
        dist_student = pair_distances(blocks[1])
        return (jnp.sum(jnp.where(off_diagonal, dist_student, 0.0)), jnp.sum(jnp.where(off_diagonal, dist_teacher, 0.0)))
    total_student, total_teacher = lax.map(first_pass, (teacher_groups, student_groups))
    mean_student = jnp.sum(total_student) / pair_count
    mean_teacher = jnp.sum(total_teacher) / pair_count

    def slope_terms(blocks):
        dist_teacher = pair_distances(blocks[0])
        dist_student = pair_distances(blocks[1])
        errors = dist_student / mean_student - dist_teacher / mean_teacher
        return (dist_student, errors)

    def second_pass(blocks):
        dist_student, errors = slope_terms(blocks)
        slopes = jnp.clip(errors, -1.0, 1.0)
        huber_terms = jnp.where(jnp.abs(errors) < 1.0, 0.5 * errors * errors, jnp.abs(errors) - 0.5)
        return (jnp.sum(jnp.where(off_diagonal, slopes * dist_student, 0.0)), jnp.sum(jnp.where(off_diagonal, huber_terms, 0.0)))
    curvatures, huber_sums = lax.map(second_pass, (teacher_groups, student_groups))
    factor = jnp.sum(curvatures) / (pair_count * mean_student * mean_student)

    def third_pass(blocks):
        dist_student, errors = slope_terms(blocks)
        slopes = jnp.clip(errors, -1.0, 1.0)
        weights = jnp.where(off_diagonal, (slopes / mean_student - factor) / dist_student, 0.0).astype(jnp.bfloat16)
        row_total = lax.optimization_barrier(jnp.sum(weights.astype(jnp.float32), 1))
        return blocks[1].astype(jnp.float32) * row_total[:, None] - jnp.dot(weights, blocks[1], preferred_element_type=jnp.float32)
    gradient = lax.map(third_pass, (teacher_groups, student_groups)).reshape(TOTAL, DS)
    return (gradient, jnp.sum(huber_sums) / pair_count)
```

```python
import functools
import jax
import jax.numpy as jnp
from jax import lax
from jax.experimental import pallas as pl
from jax.experimental.pallas import tpu as pltpu
from jax.sharding import PartitionSpec as P

MESH = pl.DeviceIdType.MESH
F32 = jnp.float32
NY = 8
NZ = 4
NP = 8
NT = (((1,), (1,)), ((), ()))


def fold(values):
    rows, columns = values.shape
    part = jnp.sum(values.reshape(rows // 8, 8, columns), 0)
    total = part[:, 0:128]
    for k in range(1, columns // 128):
        total = total + part[:, k * 128 : (k + 1) * 128]
    return total


def kernel(
    pair_count,
    t_ref, s_ref, grad_ref, loss_ref,
    ti, si, tj, sj,
    dist_t, dist_s, inv_s, norm_t, norm_s,
    w_ij, w_ji, part_i, part_j,
    in_yr, in_yl, in_zr, in_zl,
    sums,
    send_y, recv_y, send_z, recv_z,
    send_sum, recv_sum,
    send_gy, recv_gy, send_gz, recv_gz,
):
    rows, dt = t_ref.shape
    ds = s_ref.shape[1]
    half = rows // 2
    cut = part_j.shape[1]
    group = lax.axis_index("group")
    blk = lax.axis_index("blk")
    b, c = blk // NY, lax.rem(blk, NY)
    core, rest = lax.rem(group, 2), group // 2
    zc = b * 2 + core

    def y_device(index):
        return (group, b * NY + index)

    def zc_device(index):
        return (rest * 2 + lax.rem(index, 2), (index // 2) * NY + c)

    def rest_device(index):
        return (index * 2 + core, blk)

    stages = ((y_device, c), (zc_device, zc), (rest_device, rest))

    barrier = pltpu.get_barrier_semaphore()
    for device, me in stages:
        for j in range(1, NP):
            pl.semaphore_signal(
                barrier, inc=1, device_id=device(lax.rem(me + j, NP)), device_id_type=MESH
            )
    ti[0:rows] = t_ref[...]
    si[0:rows] = s_ref[...]
    tj[0:rows] = t_ref[...]
    sj[0:rows] = s_ref[...]
    pl.semaphore_wait(barrier, 3 * (NP - 1))

    y_right, y_left = y_device(lax.rem(c + 1, NY)), y_device(lax.rem(c + NY - 1, NY))
    z_right = (group, lax.rem(blk + NY, NY * NZ))
    z_left = (group, lax.rem(blk + NY * (NZ - 1), NY * NZ))

    def slot(k):
        return pl.ds(k * rows, rows)

    def y_copy(what, src, dst, to):
        ref = (si, ti)[what]
        return pltpu.make_async_remote_copy(
            src_ref=ref.at[slot(src)], dst_ref=ref.at[slot(dst)],
            send_sem=send_y.at[what, dst], recv_sem=recv_y.at[what, dst],
            device_id=to, device_id_type=MESH,
        )

    def z_copy(what, src, dst, to, way):
        ref = (sj, tj)[what]
        return pltpu.make_async_remote_copy(
            src_ref=ref.at[slot(src)], dst_ref=ref.at[slot(dst)],
            send_sem=send_z.at[what, way, dst], recv_sem=recv_z.at[what, dst],
            device_id=to, device_id_type=MESH,
        )

    def z_wait(what, dst):
        z_copy(what, 0, dst, z_right, 0).wait_recv()

    for what in range(2):
        y_copy(what, 0, 7, y_right).start()
        y_copy(what, 0, 1, y_left).start()

        @pl.when(b < 3)
        def _():
            z_copy(what, 0, 3, z_right, 0).start()

        @pl.when(b > 0)
        def _():
            z_copy(what, 0, 1, z_left, 1).start()

    for what in range(2):
        y_copy(what, 0, 7, y_right).wait_recv()
        y_copy(what, 7, 6, y_right).start()
        y_copy(what, 0, 1, y_left).wait_recv()
        y_copy(what, 1, 2, y_left).start()

        @pl.when(b >= 1)
        def _():
            z_wait(what, 3)

        @pl.when((b >= 1) & (b < 3))
        def _():
            z_copy(what, 3, 2, z_right, 0).start()

        @pl.when(b <= 2)
        def _():
            z_wait(what, 1)

        @pl.when((b <= 2) & (b > 0))
        def _():
            z_copy(what, 1, 2, z_left, 1).start()

    for what in range(2):
        y_copy(what, 7, 6, y_right).wait_recv()
        y_copy(what, 6, 5, y_right).start()
        y_copy(what, 1, 2, y_left).wait_recv()
        y_copy(what, 2, 3, y_left).start()
        z_wait(what, 2)

        @pl.when(b == 2)
        def _():
            z_copy(what, 2, 1, z_right, 0).start()

        @pl.when(b == 1)
        def _():
            z_copy(what, 2, 3, z_left, 1).start()

    y_copy(0, 2, 3, y_left).wait_recv()
    y_copy(0, 3, 4, y_left).start()
    y_copy(0, 6, 5, y_right).wait_recv()
    y_copy(1, 6, 5, y_right).wait_recv()
    y_copy(1, 5, 4, y_right).start()
    y_copy(1, 2, 3, y_left).wait_recv()

    for what in range(2):

        @pl.when(b == 0)
        def _():
            z_wait(what, 3)

        @pl.when(b == 3)
        def _():
            z_wait(what, 1)

    for ref, norm in ((tj, norm_t), (sj, norm_s)):
        for k in range(NZ):
            wide = ref[slot(k)].astype(F32)
            squares = jnp.sum(wide * wide, 1, keepdims=True)
            turned = jnp.transpose(jnp.broadcast_to(squares, (rows, 128)))
            norm[:, k * rows : (k + 1) * rows] = turned[0:8]

    def distance(ref, other, norm, place):
        own = ref[place]
        wide = own.astype(F32)
        squares = jnp.sum(wide * wide, 1, keepdims=True)
        products = lax.dot_general(own, other[...], NT, preferred_element_type=F32)
        spread = squares + norm[0:1] - 2.0 * products
        return jnp.sqrt(jnp.maximum(spread, 0.0) + 1.0)

    def first_pass(k, diagonal):
        place = pl.ds(pl.multiple_of(k * rows, rows), rows)
        near_t = distance(ti, tj, norm_t, place)
        near_s = distance(si, sj, norm_s, place)
        inverse = 1.0 / near_s
        if diagonal:
            at = lax.broadcasted_iota(jnp.int32, near_s.shape, 0)
            off = at != lax.broadcasted_iota(jnp.int32, near_s.shape, 1)
            near_t = jnp.where(off, near_t, 0.0)
            near_s = jnp.where(off, near_s, 0.0)
            inverse = jnp.where(off, inverse, 0.0)
        dist_t[place] = near_t
        dist_s[place] = near_s
        inv_s[place] = inverse
        return fold(near_s), fold(near_t)

    def add_pass(total, more):
        return total[0] + more[0], total[1] + more[1]

    total = first_pass(0, True)
    total = lax.fori_loop(1, 4, lambda k, now: add_pass(now, first_pass(k, False)), total)
    total = lax.fori_loop(5, 8, lambda k, now: add_pass(now, first_pass(k, False)), total)
    y_copy(0, 3, 4, y_left).wait_recv()
    y_copy(1, 5, 4, y_right).wait_recv()
    total = add_pass(total, first_pass(4, False))

    def sum_all(which, pair):
        one, two = (jnp.sum(tile, 0, keepdims=True) for tile in pair)
        first = lax.broadcasted_iota(jnp.int32, (8, 128), 0) == 0
        tile = jnp.where(first, one, two)
        for stage, (device, me) in enumerate(stages):
            at = which * 3 + stage
            sums[at, me] = tile

            def copy(j):
                return pltpu.make_async_remote_copy(
                    src_ref=sums.at[at, me], dst_ref=sums.at[at, me],
                    send_sem=send_sum.at[at, j], recv_sem=recv_sum.at[at, me],
                    device_id=device(lax.rem(me + j, NP)), device_id_type=MESH,
                )

            for j in range(1, NP):
                copy(j).start()
            for j in range(1, NP):
                peer = lax.rem(me + j, NP)
                pltpu.make_async_remote_copy(
                    src_ref=sums.at[at, peer], dst_ref=sums.at[at, peer],
                    send_sem=send_sum.at[at, j], recv_sem=recv_sum.at[at, peer],
                    device_id=device(peer), device_id_type=MESH,
                ).wait_recv()
            tile = sums[at, 0]
            for j in range(1, NP):
                tile = tile + sums[at, j]
            for j in range(1, NP):
                copy(j).wait_send()
        wide = jnp.sum(tile, 1, keepdims=True)
        return wide[0:1], wide[1:2]

    total_s, total_t = sum_all(0, total)
    scale_s = pair_count / total_s
    scale_t = pair_count / total_t

    def second_pass(k, now):
        place = pl.ds(pl.multiple_of(k * rows, rows), rows)
        near_s = dist_s[place]
        error = near_s * scale_s - dist_t[place] * scale_t
        slope = jnp.clip(error, -1.0, 1.0)
        dist_t[place] = slope
        return now[0] + fold(slope * near_s), now[1] + fold(slope * (error - 0.5 * slope))

    zero = jnp.zeros((8, 128), F32)
    curvature, huber = sum_all(1, lax.fori_loop(0, NY, second_pass, (zero, zero)))
    loss_ref[...] = jnp.broadcast_to(huber / pair_count, (8, 128))
    factor = curvature * scale_s * scale_s / pair_count

    def third_pass(k, carry):
        start = pl.multiple_of(k * rows, rows)
        place = pl.ds(start, rows)
        weight = (dist_t[place] * scale_s - factor) * inv_s[place]
        w_ij[place] = weight.astype(jnp.bfloat16)
        w_ji[:, place] = jnp.transpose(weight).astype(jnp.bfloat16)
        return carry

    lax.fori_loop(0, NY, third_pass, 0)

    def make_i(k):
        weight = w_ij[slot(k)]
        count = jnp.sum(weight.astype(F32), 1, keepdims=True)
        part_i[slot(k)] = si[slot(k), cut:ds].astype(F32) * count - jnp.dot(
            weight, sj[:, cut:ds], preferred_element_type=F32
        )

    def make_j(k):
        weight = w_ji[slot(k)]
        count = jnp.sum(weight.astype(F32), 1, keepdims=True)
        part_j[slot(k)] = sj[slot(k), 0:cut].astype(F32) * count - jnp.dot(
            weight, si[:, 0:cut], preferred_element_type=F32
        )

    def gy_copy(way, m, piece):
        k = m if way == 0 else (NY - m) % NY
        return pltpu.make_async_remote_copy(
            src_ref=part_i.at[pl.ds(k * rows + piece * half, half)],
            dst_ref=(in_yr, in_yl)[way].at[m - 1, piece],
            send_sem=send_gy.at[way, m - 1, piece], recv_sem=recv_gy.at[way, m - 1, piece],
            device_id=(y_right, y_left)[way], device_id_type=MESH,
        )

    def gy_add(way, m, piece):
        gy_copy(way, m + 1, piece).wait_recv()
        k = m if way == 0 else (NY - m) % NY
        place = pl.ds(k * rows + piece * half, half)
        part_i[place] = part_i[place] + (in_yr, in_yl)[way][m, piece]

    def gz_copy(way, m, piece):
        k = m if way == 0 else (NZ - m) % NZ
        return pltpu.make_async_remote_copy(
            src_ref=part_j.at[pl.ds(k * rows + piece * half, half)],
            dst_ref=(in_zr, in_zl)[way].at[m - 1, piece],
            send_sem=send_gz.at[way, m - 1, piece], recv_sem=recv_gz.at[way, m - 1, piece],
            device_id=(z_right, z_left)[way], device_id_type=MESH,
        )

    def gz_add(way, m, piece):
        gz_copy(way, m + 1, piece).wait_recv()
        k = m if way == 0 else (NZ - m) % NZ
        place = pl.ds(k * rows + piece * half, half)
        part_j[place] = part_j[place] + (in_zr, in_zl)[way][m, piece]

    def gz_sends(way, m):
        sends = (b + m <= NZ - 1) if way == 0 else (b - m >= 0)
        comes = (b >= 1) if way == 0 else (b <= NZ - 2)
        return sends, sends & comes

    def gz_round(m, add):
        for piece in range(2):
            for way in range(2):
                sends, comes = gz_sends(way, m)
                if add:

                    @pl.when(comes)
                    def _():
                        gz_add(way, m, piece)

                @pl.when(sends)
                def _():
                    gz_copy(way, m, piece).start()

    make_i(4)
    gy_copy(0, 4, 0).start()
    gy_copy(1, 4, 1).start()
    make_j(3)
    make_j(1)
    gz_round(3, False)
    make_i(3)
    make_i(5)
    gy_copy(0, 3, 1).start()
    gy_copy(1, 3, 0).start()
    make_j(2)
    make_i(2)
    make_i(6)
    make_i(1)
    make_i(7)
    make_i(0)
    make_j(0)

    gy_add(0, 3, 0)
    gy_copy(0, 3, 0).start()
    gy_add(1, 3, 1)
    gy_copy(1, 3, 1).start()
    gz_round(2, True)
    for m in (2, 1):
        for piece in range(2):
            for way in range(2):
                order = 1 - piece if way == 0 else piece
                gy_add(way, m, order)
                gy_copy(way, m, order).start()
        if m == 2:
            gz_round(1, True)

    for piece in range(2):
        for way in range(2):
            sends, comes = gz_sends(way, 0)

            @pl.when(comes)
            def _():
                gz_add(way, 0, piece)

    for piece in range(2):
        for way in range(2):
            gy_add(way, 0, 1 - piece if way == 0 else piece)
    grad_ref[:, 0:cut] = part_j[0:rows]
    grad_ref[:, cut:ds] = part_i[0:rows]

    for what in range(2):
        for src, dst, to in ((0, 7, y_right), (0, 1, y_left), (7, 6, y_right), (1, 2, y_left),
                             (6, 5, y_right), (2, 3, y_left)):
            y_copy(what, src, dst, to).wait_send()
        for cond, src, dst, to, way in (
            (b < 3, 0, 3, z_right, 0), (b > 0, 0, 1, z_left, 1),
            ((b >= 1) & (b < 3), 3, 2, z_right, 0), ((b <= 2) & (b > 0), 1, 2, z_left, 1),
            (b == 2, 2, 1, z_right, 0), (b == 1, 2, 3, z_left, 1),
        ):

            @pl.when(cond)
            def _():
                z_copy(what, src, dst, to, way).wait_send()

    y_copy(0, 3, 4, y_left).wait_send()
    y_copy(1, 5, 4, y_right).wait_send()
    for way in range(2):
        gy_copy(way, 4, way).wait_send()
        for m in (3, 2, 1):
            for piece in range(2):
                gy_copy(way, m, piece).wait_send()
            sends, _ = gz_sends(way, m)

            @pl.when(sends)
            def _():
                for piece in range(2):
                    gz_copy(way, m, piece).wait_send()


def shards(teacher, student):
    rows, dt = teacher.shape
    ds = student.shape[1]
    batch_rows = rows * lax.axis_size("blk")
    pair_count = 1.0 * lax.axis_size("group") * batch_rows * (batch_rows - 1)
    cut = ds // 2
    ni, nj = NY * rows, NZ * rows
    bf16 = jnp.bfloat16
    vmem, dma = pltpu.VMEM, pltpu.SemaphoreType.DMA
    gradient, loss = pl.pallas_call(
        functools.partial(kernel, pair_count),
        out_shape=(
            jax.ShapeDtypeStruct((rows, ds), F32),
            jax.ShapeDtypeStruct((8, 128), F32),
        ),
        in_specs=[pl.BlockSpec(memory_space=vmem)] * 2,
        out_specs=[pl.BlockSpec(memory_space=vmem)] * 2,
        scratch_shapes=[
            vmem((ni, dt), bf16), vmem((ni, ds), bf16), vmem((nj, dt), bf16), vmem((nj, ds), bf16),
            vmem((ni, nj), F32), vmem((ni, nj), F32), vmem((ni, nj), F32),
            vmem((8, nj), F32), vmem((8, nj), F32),
            vmem((ni, nj), bf16), vmem((nj, ni), bf16),
            vmem((ni, ds - cut), F32), vmem((nj, cut), F32),
            vmem((4, 2, rows // 2, ds - cut), F32), vmem((4, 2, rows // 2, ds - cut), F32),
            vmem((3, 2, rows // 2, cut), F32), vmem((3, 2, rows // 2, cut), F32),
            vmem((6, NP, 8, 128), F32),
            dma((2, NY)), dma((2, NY)), dma((2, 2, NZ)), dma((2, NZ)),
            dma((6, NP)), dma((6, NP)),
            dma((2, 4, 2)), dma((2, 4, 2)), dma((2, 3, 2)), dma((2, 3, 2)),
        ],
        compiler_params=pltpu.CompilerParams(
            collective_id=0, has_side_effects=True, vmem_limit_bytes=50 * 1024 * 1024
        ),
    )(teacher, student)
    return (gradient, loss[0, 0])


def solution(mesh):
    in_specs = (P(("group", "blk"), None), P(("group", "blk"), None))
    out_specs = (P(("group", "blk"), None), P())
    return jax.shard_map(shards, mesh=mesh, in_specs=in_specs, out_specs=out_specs, check_vma=False)
```

```python
import functools
import jax
import jax.numpy as jnp
from jax import lax
from jax.experimental import pallas as pl
from jax.experimental.pallas import tpu as pltpu
from jax.sharding import PartitionSpec as P

MESH = pl.DeviceIdType.MESH
F32 = jnp.float32
NY = 8
NZ = 4
NX = 4
NP = 8
NT = (((1,), (1,)), ((), ()))


def fold(values):
    rows, columns = values.shape
    part = jnp.sum(values.reshape(rows // 8, 8, columns), 0)
    total = part[:, 0:128]
    for k in range(1, columns // 128):
        total = total + part[:, k * 128 : (k + 1) * 128]
    return total


def kernel(
    pair_count,
    t_ref, s_ref, grad_ref, loss_ref,
    ti, si, tj, sj,
    dist_t, dist_s, inv_s, norm_t, norm_s, own_t, own_s,
    w_ij, w_ji, part_i, part_j,
    in_yr, in_yl, in_zr, in_zl,
    sums,
    load, send_y, recv_y, send_z, recv_z,
    send_sum, recv_sum,
    send_gy, recv_gy, send_gz, recv_gz,
    inside,
):
    rows = t_ref.shape[0]
    ds = s_ref.shape[1]
    half = rows // 2
    cut = part_j.shape[1]
    group = lax.axis_index("group")
    blk = lax.axis_index("blk")
    b, c = blk // NY, lax.rem(blk, NY)
    core, x = lax.rem(group, 2), lax.rem(group // 2, NX)
    z = (group // (2 * NX)) * NZ + b
    xc = x * 2 + core

    def device(z, x, core, y):
        return ((z // NZ * NX + x) * 2 + core, lax.rem(z, NZ) * NY + y)

    def y_device(index):
        return device(z, x, core, index)

    def z_device(index):
        return device(index, x, core, c)

    def xc_device(index):
        return device(z, index // 2, lax.rem(index, 2), c)

    stages = ((y_device, c), (z_device, z), (xc_device, xc))

    y_right, y_left = y_device(lax.rem(c + 1, NY)), y_device(lax.rem(c + NY - 1, NY))
    z_right, z_left = z_device(lax.rem(z + 1, NP)), z_device(lax.rem(z + NP - 1, NP))
    near = (
        y_right, y_left, z_right, z_left,
        device(z, lax.rem(x + 1, NX), core, c), device(z, lax.rem(x + NX - 1, NX), core, c),
        device(z, x, 1 - core, c),
    )

    barrier = pltpu.get_barrier_semaphore()
    for other in near:
        pl.semaphore_signal(barrier, inc=1, device_id=other, device_id_type=MESH)

    def slot(k):
        return pl.ds(k * rows, rows)

    loads = [
        pltpu.make_async_copy(src, dst.at[slot(0)], load.at[n])
        for n, (src, dst) in enumerate(((s_ref, si), (s_ref, sj), (t_ref, ti), (t_ref, tj)))
    ]
    for copy in loads:
        copy.start()
    for copy in loads:
        copy.wait()
    pl.semaphore_wait(barrier, len(near))

    def round_signal(r):
        for other in near:
            pl.semaphore_signal(inside.at[r], inc=1, device_id=other, device_id_type=MESH)

    def round_wait(r):
        pl.semaphore_wait(inside.at[r], len(near))

    y_up = y_device(lax.rem(c + jnp.where(core == 0, 1, NY - 1), NY))
    y_down = y_device(lax.rem(c + jnp.where(core == 0, NY - 1, 1), NY))

    def piece_of(refs, k, piece):
        return refs[piece // 2].at[pl.ds(k * rows + (piece % 2) * half, half)]

    def y_copy(piece, src, dst, to):
        return pltpu.make_async_remote_copy(
            src_ref=piece_of((si, ti), src, piece), dst_ref=piece_of((si, ti), dst, piece),
            send_sem=send_y.at[piece, dst], recv_sem=recv_y.at[piece, dst],
            device_id=to, device_id_type=MESH,
        )

    def place(k, b):
        last = jnp.where(b == 0, 3, jnp.where(b == 3, 1, 2))
        return jnp.where(last == k, 3, last if k == 3 else k)

    def z_piece(k, b, piece):
        start = pl.multiple_of(place(k, b) * rows + (piece % 2) * half, half)
        return (sj, tj)[piece // 2].at[pl.ds(start, half)]

    def z_copy(piece, src, dst, to, way):
        return pltpu.make_async_remote_copy(
            src_ref=z_piece(src, b, piece), dst_ref=z_piece(dst, b + (1, -1)[way], piece),
            send_sem=send_z.at[piece, way, dst], recv_sem=recv_z.at[piece, dst],
            device_id=to, device_id_type=MESH,
        )

    def z_wait(piece, dst):
        pltpu.make_async_remote_copy(
            src_ref=z_piece(0, b, piece), dst_ref=z_piece(dst, b, piece),
            send_sem=send_z.at[piece, 0, dst], recv_sem=recv_z.at[piece, dst],
            device_id=z_right, device_id_type=MESH,
        ).wait_recv()

    def y_early(k):
        for piece in range(4):
            if k > 0:
                y_copy(piece, k - 1, k, y_down).wait_recv()
            if k < 4:
                y_copy(piece, k, k + 1, y_down).start()

    def y_late(k):
        for piece in range(4):
            if k > 0:
                y_copy(piece, (NY + 1 - k) % NY, NY - k, y_up).wait_recv()
            if k < 3:
                y_copy(piece, (NY - k) % NY, NY - k - 1, y_up).start()

    def z_step(k):
        for piece in range(4):
            if k == 0:

                @pl.when(b < 3)
                def _():
                    z_copy(piece, 0, 3, z_right, 0).start()

                @pl.when(b > 0)
                def _():
                    z_copy(piece, 0, 1, z_left, 1).start()

            if k == 1:

                @pl.when(b >= 1)
                def _():
                    z_wait(piece, 3)

                @pl.when((b >= 1) & (b < 3))
                def _():
                    z_copy(piece, 3, 2, z_right, 0).start()

                @pl.when(b <= 2)
                def _():
                    z_wait(piece, 1)

                @pl.when((b <= 2) & (b > 0))
                def _():
                    z_copy(piece, 1, 2, z_left, 1).start()

            if k == 2:
                z_wait(piece, 2)

                @pl.when(b == 2)
                def _():
                    z_copy(piece, 2, 1, z_right, 0).start()

                @pl.when(b == 1)
                def _():
                    z_copy(piece, 2, 3, z_left, 1).start()

            if k == 3:

                @pl.when(b == 0)
                def _():
                    z_wait(piece, 3)

                @pl.when(b == 3)
                def _():
                    z_wait(piece, 1)

    def squares_of(values):
        wide = values.astype(F32)
        return jnp.sum(wide * wide, 1, keepdims=True)

    def norms_j(k):
        for ref, norm in ((tj, norm_t), (sj, norm_s)):
            squares = squares_of(ref[slot(k)])
            norm[:, k * rows : (k + 1) * rows] = jnp.transpose(jnp.broadcast_to(squares, (rows, 128)))[0:8]

    def norms_i(at):
        for ref, norm in ((ti, own_t), (si, own_s)):
            own = ref[at]
            norm[at] = jnp.broadcast_to(squares_of(own), (own.shape[0], 128))

    def distance(ref, other, own_norm, norm, at, lo, hi):
        products = lax.dot_general(ref[at], other[lo:hi], NT, preferred_element_type=F32)
        spread = own_norm[at][:, 0:1] + norm[0:1, lo:hi] - 2.0 * products
        return jnp.sqrt(jnp.maximum(spread, 0.0) + 1.0)

    def distances(at, lo, hi, diagonal):
        near_t = distance(ti, tj, own_t, norm_t, at, lo, hi)
        near_s = distance(si, sj, own_s, norm_s, at, lo, hi)
        inverse = 1.0 / near_s
        if diagonal:
            row = lax.broadcasted_iota(jnp.int32, near_s.shape, 0)
            off = row != lax.broadcasted_iota(jnp.int32, near_s.shape, 1)
            near_t = jnp.where(off, near_t, 0.0)
            near_s = jnp.where(off, near_s, 0.0)
            inverse = jnp.where(off, inverse, 0.0)
        dist_t[at, lo:hi] = near_t
        dist_s[at, lo:hi] = near_s
        inv_s[at, lo:hi] = inverse
        return near_s, near_t

    def first_pass(k):
        norms_i(slot(k))
        times = 2.0 if 1 <= k <= 3 else 1.0
        return [times * fold(near) for near in distances(slot(k), 0, 3 * rows, k == 0)]

    def add(one, two):
        return [a + b for a, b in zip(one, two)]

    y_early(0)
    z_step(0)
    round_signal(0)
    y_early(1)
    round_wait(0)
    round_signal(1)
    y_early(2)
    z_step(1)
    round_wait(1)
    round_signal(2)
    y_early(3)
    y_late(0)
    norms_j(0)
    y_early(4)
    z_step(2)
    round_wait(2)
    norms_j(1)
    norms_j(2)
    total = first_pass(0)
    total = add(total, first_pass(1))
    y_late(1)
    total = add(total, first_pass(2))
    total = add(total, first_pass(3))
    y_late(2)
    total = add(total, first_pass(4))
    z_step(3)
    norms_j(3)

    def last_pass(start, count, times):
        near = distances(pl.ds(start * rows, count * rows), 3 * rows, 4 * rows, False)
        return [times * fold(one) for one in near]

    total = add(total, last_pass(0, 1, 1.0))
    total = add(total, last_pass(1, 3, 2.0))
    total = add(total, last_pass(4, 1, 1.0))

    def sum_all(which, pair, meanwhile):
        one, two = (jnp.sum(tile, 0, keepdims=True) for tile in pair)
        first = lax.broadcasted_iota(jnp.int32, (8, 128), 0) == 0
        tile = jnp.where(first, one, two)
        for stage, (where, me) in enumerate(stages):
            at = which * 3 + stage
            sums[at, me] = tile

            def copy(j, row):
                return pltpu.make_async_remote_copy(
                    src_ref=sums.at[at, row], dst_ref=sums.at[at, row],
                    send_sem=send_sum.at[at, j], recv_sem=recv_sum.at[at, row],
                    device_id=where(lax.rem(me + j, NP)), device_id_type=MESH,
                )

            for j in (4, 3, 5, 2, 6, 1, 7):
                copy(j, me).start()
            meanwhile[stage]()
            for j in range(1, NP):
                copy(j, lax.rem(me + j, NP)).wait_recv()
            tile = sums[at, 0]
            for j in range(1, NP):
                tile = tile + sums[at, j]
            for j in range(1, NP):
                copy(j, me).wait_send()
        wide = jnp.sum(tile, 1, keepdims=True)
        return wide[0:1], wide[1:2]

    def late_pass(k):
        norms_i(slot(k))
        distances(slot(k), 0, NZ * rows, False)

    def late_last():
        y_late(3)
        late_pass(5)

    def nothing():
        pass

    total_s, total_t = sum_all(0, total, (lambda: late_pass(7), lambda: late_pass(6), late_last))
    scale_s = pair_count / total_s
    scale_t = pair_count / total_t

    def second_pass(k, now):
        at = pl.ds(pl.multiple_of(k * rows, rows), rows)
        near_s = dist_s[at]
        error = near_s * scale_s - dist_t[at] * scale_t
        slope = jnp.clip(error, -1.0, 1.0)
        dist_t[at] = slope
        return now[0] + fold(slope * near_s), now[1] + fold(slope * (error - 0.5 * slope))

    zero = jnp.zeros((8, 128), F32)
    total = lax.fori_loop(1, 4, second_pass, (zero, zero))
    total = second_pass(0, second_pass(4, (2.0 * total[0], 2.0 * total[1])))

    def late_slopes():
        lax.fori_loop(5, NY, second_pass, (zero, zero))

    curvature, huber = sum_all(1, total, (late_slopes, nothing, nothing))
    loss_ref[...] = jnp.broadcast_to(huber / pair_count, (8, 128))
    factor = curvature * scale_s * scale_s / pair_count

    def third_pass(k, carry):
        start = pl.multiple_of(k * rows, rows)
        at = pl.ds(start, rows)
        weight = (dist_t[at] * scale_s - factor) * inv_s[at]
        w_ij[at] = weight.astype(jnp.bfloat16)
        w_ji[:, at] = jnp.transpose(weight).astype(jnp.bfloat16)
        return carry

    lax.fori_loop(0, NY, third_pass, 0)

    def make_i(k):
        weight = w_ij[slot(k)]
        count = jnp.sum(weight.astype(F32), 1, keepdims=True)
        part_i[slot(k)] = si[slot(k), cut:ds].astype(F32) * count - jnp.dot(
            weight, sj[:, cut:ds], preferred_element_type=F32
        )

    def make_j(k):
        at = pl.ds(pl.multiple_of(place(k, b) * rows, rows), rows)
        weight = w_ji[at]
        count = jnp.sum(weight.astype(F32), 1, keepdims=True)
        part_j[slot(k)] = sj[at, 0:cut].astype(F32) * count - jnp.dot(
            weight, si[:, 0:cut], preferred_element_type=F32
        )

    def gy_copy(way, m, piece):
        k = m if way == 0 else (NY - m) % NY
        return pltpu.make_async_remote_copy(
            src_ref=part_i.at[pl.ds(k * rows + piece * half, half)],
            dst_ref=(in_yr, in_yl)[way].at[m - 1, piece],
            send_sem=send_gy.at[way, m - 1, piece], recv_sem=recv_gy.at[way, m - 1, piece],
            device_id=(y_up, y_down)[way], device_id_type=MESH,
        )

    def gy_add(way, m, piece):
        gy_copy(way, m + 1, piece).wait_recv()
        k = m if way == 0 else (NY - m) % NY
        at = pl.ds(k * rows + piece * half, half)
        part_i[at] = part_i[at] + (in_yr, in_yl)[way][m, piece]

    def gz_copy(way, m, piece):
        k = m if way == 0 else (NZ - m) % NZ
        return pltpu.make_async_remote_copy(
            src_ref=part_j.at[pl.ds(k * rows + piece * half, half)],
            dst_ref=(in_zr, in_zl)[way].at[m - 1, piece],
            send_sem=send_gz.at[way, m - 1, piece], recv_sem=recv_gz.at[way, m - 1, piece],
            device_id=(z_right, z_left)[way], device_id_type=MESH,
        )

    def gz_add(way, m, piece):
        gz_copy(way, m + 1, piece).wait_recv()
        k = m if way == 0 else (NZ - m) % NZ
        at = pl.ds(k * rows + piece * half, half)
        part_j[at] = part_j[at] + (in_zr, in_zl)[way][m, piece]

    def gz_sends(way, m):
        sends = (b + m <= NZ - 1) if way == 0 else (b - m >= 0)
        comes = (b >= 1) if way == 0 else (b <= NZ - 2)
        return sends, sends & comes

    def gz_round(m, add):
        for piece in range(2):
            for way in range(2):
                sends, comes = gz_sends(way, m)
                if add:

                    @pl.when(comes)
                    def _():
                        gz_add(way, m, piece)

                @pl.when(sends)
                def _():
                    gz_copy(way, m, piece).start()

    make_i(4)
    gy_copy(0, 4, 0).start()
    gy_copy(1, 4, 1).start()
    make_j(3)
    make_j(1)
    gz_round(3, False)
    make_i(3)
    make_i(5)
    gy_copy(0, 3, 1).start()
    gy_copy(1, 3, 0).start()
    make_j(2)
    make_i(2)
    make_i(6)
    make_i(1)
    make_i(7)
    make_i(0)
    make_j(0)

    gy_add(0, 3, 0)
    gy_copy(0, 3, 0).start()
    gy_add(1, 3, 1)
    gy_copy(1, 3, 1).start()
    gz_round(2, True)
    for m in (2, 1):
        for piece in range(2):
            for way in range(2):
                order = 1 - piece if way == 0 else piece
                gy_add(way, m, order)
                gy_copy(way, m, order).start()
        if m == 2:
            gz_round(1, True)

    for piece in range(2):
        for way in range(2):
            sends, comes = gz_sends(way, 0)

            @pl.when(comes)
            def _():
                gz_add(way, 0, piece)

    for piece in range(2):
        for way in range(2):
            gy_add(way, 0, 1 - piece if way == 0 else piece)
    grad_ref[:, 0:cut] = part_j[0:rows]
    grad_ref[:, cut:ds] = part_i[0:rows]

    for piece in range(4):
        for k in range(4):
            y_copy(piece, k, k + 1, y_down).wait_send()
        for k in range(3):
            y_copy(piece, (NY - k) % NY, NY - k - 1, y_up).wait_send()
        for cond, src, dst, to, way in (
            (b < 3, 0, 3, z_right, 0), (b > 0, 0, 1, z_left, 1),
            ((b >= 1) & (b < 3), 3, 2, z_right, 0), ((b <= 2) & (b > 0), 1, 2, z_left, 1),
            (b == 2, 2, 1, z_right, 0), (b == 1, 2, 3, z_left, 1),
        ):

            @pl.when(cond)
            def _():
                z_copy(piece, src, dst, to, way).wait_send()

    for way in range(2):
        gy_copy(way, 4, way).wait_send()
        for m in (3, 2, 1):
            for piece in range(2):
                gy_copy(way, m, piece).wait_send()
            sends, _ = gz_sends(way, m)

            @pl.when(sends)
            def _():
                for piece in range(2):
                    gz_copy(way, m, piece).wait_send()


def shards(teacher, student):
    rows, dt = teacher.shape
    ds = student.shape[1]
    batch_rows = rows * lax.axis_size("blk")
    pair_count = 1.0 * lax.axis_size("group") * batch_rows * (batch_rows - 1)
    cut = ds // 2
    ni, nj = NY * rows, NZ * rows
    bf16 = jnp.bfloat16
    vmem, dma = pltpu.VMEM, pltpu.SemaphoreType.DMA
    gradient, loss = pl.pallas_call(
        functools.partial(kernel, pair_count),
        out_shape=(
            jax.ShapeDtypeStruct((rows, ds), F32),
            jax.ShapeDtypeStruct((8, 128), F32),
        ),
        in_specs=[pl.BlockSpec(memory_space=pltpu.HBM)] * 2,
        out_specs=[pl.BlockSpec(memory_space=vmem), pl.BlockSpec(memory_space=vmem)],
        scratch_shapes=[
            vmem((ni, dt), bf16), vmem((ni, ds), bf16), vmem((nj, dt), bf16), vmem((nj, ds), bf16),
            vmem((ni, nj), F32), vmem((ni, nj), F32), vmem((ni, nj), F32),
            vmem((8, nj), F32), vmem((8, nj), F32), vmem((ni, 128), F32), vmem((ni, 128), F32),
            vmem((ni, nj), bf16), vmem((nj, ni), bf16),
            vmem((ni, ds - cut), F32), vmem((nj, cut), F32),
            vmem((4, 2, rows // 2, ds - cut), F32), vmem((4, 2, rows // 2, ds - cut), F32),
            vmem((3, 2, rows // 2, cut), F32), vmem((3, 2, rows // 2, cut), F32),
            vmem((6, NP, 8, 128), F32),
            dma((4,)), dma((4, NY)), dma((4, NY)), dma((4, 2, NZ)), dma((4, NZ)),
            dma((6, NP)), dma((6, NP)),
            dma((2, 4, 2)), dma((2, 4, 2)), dma((2, 3, 2)), dma((2, 3, 2)),
            pltpu.SemaphoreType.REGULAR((3,)),
        ],
        compiler_params=pltpu.CompilerParams(
            collective_id=0, has_side_effects=True, vmem_limit_bytes=62 * 1024 * 1024
        ),
    )(teacher, student)
    return (gradient, loss[0, 0])


def solution(mesh):
    in_specs = (P(("group", "blk"), None), P(("group", "blk"), None))
    out_specs = (P(("group", "blk"), None), P())
    return jax.shard_map(shards, mesh=mesh, in_specs=in_specs, out_specs=out_specs, check_vma=False)
```

```python
import functools
import jax
import jax.numpy as jnp
from jax import lax
from jax.experimental import pallas as pl
from jax.experimental.pallas import tpu as pltpu
from jax.sharding import PartitionSpec as P

MESH = pl.DeviceIdType.MESH
F32 = jnp.float32
NY = 8
NZ = 4
SPAN = 4096.0
NX = 4
NP = 8
NT = (((1,), (1,)), ((), ()))


def fold(values):
    rows, columns = values.shape
    part = jnp.sum(values.reshape(rows // 8, 8, columns), 0)
    total = part[:, 0:128]
    for k in range(1, columns // 128):
        total = total + part[:, k * 128 : (k + 1) * 128]
    return total


def kernel(
    pair_count,
    t_ref, s_ref, grad_ref, loss_ref,
    ti, si, tj, sj,
    dist_t, dist_s, inv_s, norm_t, norm_s, own_t, own_s,
    w_ij, w_ji, part_i, part_j,
    out_y, out_z, in_y, in_z,
    sums,
    load, send_y, recv_y, send_z, recv_z,
    send_sum, recv_sum,
    send_gy, recv_gy, send_gz, recv_gz,
    inside,
):
    rows = t_ref.shape[0]
    ds = s_ref.shape[1]
    half = rows // 2
    cut = part_j.shape[2]
    group = lax.axis_index("group")
    blk = lax.axis_index("blk")
    b, c = blk // NY, lax.rem(blk, NY)
    core, x = lax.rem(group, 2), lax.rem(group // 2, NX)
    z = (group // (2 * NX)) * NZ + b
    xc = x * 2 + core

    def device(z, x, core, y):
        return ((z // NZ * NX + x) * 2 + core, lax.rem(z, NZ) * NY + y)

    def y_device(index):
        return device(z, x, core, index)

    def z_device(index):
        return device(index, x, core, c)

    def xc_device(index):
        return device(z, index // 2, lax.rem(index, 2), c)

    stages = ((y_device, c), (z_device, z), (xc_device, xc))

    y_right, y_left = y_device(lax.rem(c + 1, NY)), y_device(lax.rem(c + NY - 1, NY))
    z_right, z_left = z_device(lax.rem(z + 1, NP)), z_device(lax.rem(z + NP - 1, NP))
    near = (
        y_right, y_left, z_right, z_left,
        device(z, lax.rem(x + 1, NX), core, c), device(z, lax.rem(x + NX - 1, NX), core, c),
        device(z, x, 1 - core, c),
    )

    barrier = pltpu.get_barrier_semaphore()
    for other in near:
        pl.semaphore_signal(barrier, inc=1, device_id=other, device_id_type=MESH)

    def slot(k):
        return pl.ds(k * rows, rows)

    loads = [
        pltpu.make_async_copy(src, dst.at[slot(0)], load.at[n])
        for n, (src, dst) in enumerate(((s_ref, si), (s_ref, sj), (t_ref, ti), (t_ref, tj)))
    ]
    for copy in loads:
        copy.start()
    for copy in loads:
        copy.wait()
    pl.semaphore_wait(barrier, len(near))

    def round_signal(r):
        for other in near:
            pl.semaphore_signal(inside.at[r], inc=1, device_id=other, device_id_type=MESH)

    def round_wait(r):
        pl.semaphore_wait(inside.at[r], len(near))

    y_up = y_device(lax.rem(c + jnp.where(core == 0, 1, NY - 1), NY))
    y_down = y_device(lax.rem(c + jnp.where(core == 0, NY - 1, 1), NY))

    def piece_of(refs, k, piece):
        return refs[piece // 2].at[pl.ds(k * rows + (piece % 2) * half, half)]

    def y_copy(piece, src, dst, to):
        return pltpu.make_async_remote_copy(
            src_ref=piece_of((si, ti), src, piece), dst_ref=piece_of((si, ti), dst, piece),
            send_sem=send_y.at[piece, dst], recv_sem=recv_y.at[piece, dst],
            device_id=to, device_id_type=MESH,
        )

    def place(k, b):
        last = jnp.where(b == 0, 3, jnp.where(b == 3, 1, 2))
        return jnp.where(last == k, 3, last if k == 3 else k)

    def z_piece(k, b, piece):
        start = pl.multiple_of(place(k, b) * rows + (piece % 2) * half, half)
        return (sj, tj)[piece // 2].at[pl.ds(start, half)]

    def z_copy(piece, src, dst, to, way):
        return pltpu.make_async_remote_copy(
            src_ref=z_piece(src, b, piece), dst_ref=z_piece(dst, b + (1, -1)[way], piece),
            send_sem=send_z.at[piece, way, dst], recv_sem=recv_z.at[piece, dst],
            device_id=to, device_id_type=MESH,
        )

    def z_wait(piece, dst):
        pltpu.make_async_remote_copy(
            src_ref=z_piece(0, b, piece), dst_ref=z_piece(dst, b, piece),
            send_sem=send_z.at[piece, 0, dst], recv_sem=recv_z.at[piece, dst],
            device_id=z_right, device_id_type=MESH,
        ).wait_recv()

    def y_early(k):
        for piece in range(4):
            if k > 0:
                y_copy(piece, k - 1, k, y_down).wait_recv()
            if k < 4:
                y_copy(piece, k, k + 1, y_down).start()

    def y_late(k):
        for piece in range(4):
            if k > 0:
                y_copy(piece, (NY + 1 - k) % NY, NY - k, y_up).wait_recv()
            if k < 3:
                y_copy(piece, (NY - k) % NY, NY - k - 1, y_up).start()

    def z_step(k):
        for piece in range(4):
            if k == 0:

                @pl.when(b < 3)
                def _():
                    z_copy(piece, 0, 3, z_right, 0).start()

                @pl.when(b > 0)
                def _():
                    z_copy(piece, 0, 1, z_left, 1).start()

            if k == 1:

                @pl.when(b >= 1)
                def _():
                    z_wait(piece, 3)

                @pl.when((b >= 1) & (b < 3))
                def _():
                    z_copy(piece, 3, 2, z_right, 0).start()

                @pl.when(b <= 2)
                def _():
                    z_wait(piece, 1)

                @pl.when((b <= 2) & (b > 0))
                def _():
                    z_copy(piece, 1, 2, z_left, 1).start()

            if k == 2:
                z_wait(piece, 2)

                @pl.when(b == 2)
                def _():
                    z_copy(piece, 2, 1, z_right, 0).start()

                @pl.when(b == 1)
                def _():
                    z_copy(piece, 2, 3, z_left, 1).start()

            if k == 3:

                @pl.when(b == 0)
                def _():
                    z_wait(piece, 3)

                @pl.when(b == 3)
                def _():
                    z_wait(piece, 1)

    def squares_of(values):
        wide = values.astype(F32)
        return jnp.sum(wide * wide, 1, keepdims=True)

    def norms_j(k):
        for ref, norm in ((tj, norm_t), (sj, norm_s)):
            squares = squares_of(ref[slot(k)])
            norm[:, k * rows : (k + 1) * rows] = jnp.transpose(jnp.broadcast_to(squares, (rows, 128)))[0:8]

    def norms_i(at):
        for ref, norm in ((ti, own_t), (si, own_s)):
            own = ref[at]
            norm[at] = jnp.broadcast_to(squares_of(own), (own.shape[0], 128))

    def distance(ref, other, own_norm, norm, at, lo, hi):
        products = lax.dot_general(ref[at], other[lo:hi], NT, preferred_element_type=F32)
        spread = own_norm[at][:, 0:1] + norm[0:1, lo:hi] - 2.0 * products
        return jnp.sqrt(jnp.maximum(spread, 0.0) + 1.0)

    def distances(at, lo, hi, diagonal):
        near_t = distance(ti, tj, own_t, norm_t, at, lo, hi)
        near_s = distance(si, sj, own_s, norm_s, at, lo, hi)
        inverse = 1.0 / near_s
        if diagonal:
            row = lax.broadcasted_iota(jnp.int32, near_s.shape, 0)
            off = row != lax.broadcasted_iota(jnp.int32, near_s.shape, 1)
            near_t = jnp.where(off, near_t, 0.0)
            near_s = jnp.where(off, near_s, 0.0)
            inverse = jnp.where(off, inverse, 0.0)
        dist_t[at, lo:hi] = near_t
        dist_s[at, lo:hi] = near_s
        inv_s[at, lo:hi] = inverse
        return near_s, near_t

    def first_pass(k):
        norms_i(slot(k))
        times = 2.0 if 1 <= k <= 3 else 1.0
        return [times * fold(near) for near in distances(slot(k), 0, 3 * rows, k == 0)]

    def add(one, two):
        return [a + b for a, b in zip(one, two)]

    y_early(0)
    z_step(0)
    round_signal(0)
    y_early(1)
    round_wait(0)
    round_signal(1)
    y_early(2)
    z_step(1)
    round_wait(1)
    round_signal(2)
    y_early(3)
    y_late(0)
    norms_j(0)
    y_early(4)
    z_step(2)
    round_wait(2)
    norms_j(1)
    norms_j(2)
    total = first_pass(0)
    total = add(total, first_pass(1))
    y_late(1)
    total = add(total, first_pass(2))
    total = add(total, first_pass(3))
    y_late(2)
    total = add(total, first_pass(4))
    z_step(3)
    norms_j(3)

    def last_pass(start, count, times):
        near = distances(pl.ds(start * rows, count * rows), 3 * rows, 4 * rows, False)
        return [times * fold(one) for one in near]

    total = add(total, last_pass(0, 1, 1.0))
    total = add(total, last_pass(1, 3, 2.0))
    total = add(total, last_pass(4, 1, 1.0))

    def sum_all(which, pair, meanwhile):
        one, two = (jnp.sum(tile, 0, keepdims=True) for tile in pair)
        first = lax.broadcasted_iota(jnp.int32, (8, 128), 0) == 0
        tile = jnp.where(first, one, two)
        for stage, (where, me) in enumerate(stages):
            at = which * 3 + stage
            sums[at, me] = tile

            def copy(j, row):
                return pltpu.make_async_remote_copy(
                    src_ref=sums.at[at, row], dst_ref=sums.at[at, row],
                    send_sem=send_sum.at[at, j], recv_sem=recv_sum.at[at, row],
                    device_id=where(lax.rem(me + j, NP)), device_id_type=MESH,
                )

            for j in (4, 3, 5, 2, 6, 1, 7):
                copy(j, me).start()
            meanwhile[stage]()
            for j in range(1, NP):
                copy(j, lax.rem(me + j, NP)).wait_recv()
            tile = sums[at, 0]
            for j in range(1, NP):
                tile = tile + sums[at, j]
            for j in range(1, NP):
                copy(j, me).wait_send()
        wide = jnp.sum(tile, 1, keepdims=True)
        return wide[0:1], wide[1:2]

    def late_pass(k):
        norms_i(slot(k))
        distances(slot(k), 0, NZ * rows, False)

    def keep(k, weight):
        w_ij[slot(k)] = weight.astype(jnp.bfloat16)
        w_ji[:, k * rows : (k + 1) * rows] = jnp.transpose(weight).astype(jnp.bfloat16)

    def make_i(set_, k):
        weight = w_ij[slot(k)]
        count = jnp.sum(weight.astype(F32), 1, keepdims=True)
        part_i[set_, slot(k)] = si[slot(k), cut:ds].astype(F32) * count - jnp.dot(
            weight, sj[:, cut:ds], preferred_element_type=F32
        )

    def make_j(set_, k):
        at = pl.ds(pl.multiple_of(place(k, b) * rows, rows), rows)
        weight = w_ji[at]
        count = jnp.sum(weight.astype(F32), 1, keepdims=True)
        part_j[set_, slot(k)] = sj[at, 0:cut].astype(F32) * count - jnp.dot(
            weight, si[:, 0:cut], preferred_element_type=F32
        )

    def g_at(count, way, m, piece):
        return pl.ds((m if way == 0 else (count - m) % count) * rows + piece * half, half)

    def code(out, values):
        width = values.shape[1]
        largest = jnp.max(jnp.max(jnp.abs(values), 1, keepdims=True), 0, keepdims=True)
        largest = jnp.maximum(largest, 1e-30).astype(jnp.bfloat16)
        near = values * (SPAN / largest.astype(F32))
        square = near * near
        coded = (near * jnp.abs(near) * square * (square * square)).astype(jnp.bfloat16)
        for n in range(width // 128):
            out[n * half : (n + 1) * half] = coded[:, n * 128 : (n + 1) * 128]
        out[half * (width // 128) :] = jnp.broadcast_to(largest, (16, 128))

    def decode(ref, width):
        blocks = [ref[n * half : (n + 1) * half] for n in range(width // 128)]
        coded = jnp.concatenate(blocks, 1).astype(F32)
        root = jnp.sqrt(jnp.sqrt(jnp.sqrt(jnp.abs(coded))))
        scale = ref[half * (width // 128) :].astype(F32)[0:1, 0:1] * (1.0 / SPAN)
        return jnp.where(coded < 0.0, -root, root) * scale

    def gy_copy(set_, way, m, piece):
        return pltpu.make_async_remote_copy(
            src_ref=out_y.at[set_, way, m - 1, piece], dst_ref=in_y.at[set_, way, m - 1, piece],
            send_sem=send_gy.at[set_, way, m - 1, piece], recv_sem=recv_gy.at[set_, way, m - 1, piece],
            device_id=(y_up, y_down)[way], device_id_type=MESH,
        )

    def gy_send(set_, way, m, piece):
        code(out_y.at[set_, way, m - 1, piece], part_i[set_, g_at(NY, way, m, piece)])
        gy_copy(set_, way, m, piece).start()

    def gy_add(set_, way, m, piece):
        gy_copy(set_, way, m + 1, piece).wait_recv()
        at = g_at(NY, way, m, piece)
        part_i[set_, at] = part_i[set_, at] + decode(in_y.at[set_, way, m, piece], ds - cut)

    def gz_copy(set_, way, m, piece):
        return pltpu.make_async_remote_copy(
            src_ref=out_z.at[set_, way, m - 1, piece], dst_ref=in_z.at[set_, way, m - 1, piece],
            send_sem=send_gz.at[set_, way, m - 1, piece], recv_sem=recv_gz.at[set_, way, m - 1, piece],
            device_id=(z_right, z_left)[way], device_id_type=MESH,
        )

    def gz_send(set_, way, m, piece):
        code(out_z.at[set_, way, m - 1, piece], part_j[set_, g_at(NZ, way, m, piece)])
        gz_copy(set_, way, m, piece).start()

    def gz_add(set_, way, m, piece):
        gz_copy(set_, way, m + 1, piece).wait_recv()
        at = g_at(NZ, way, m, piece)
        part_j[set_, at] = part_j[set_, at] + decode(in_z.at[set_, way, m, piece], cut)

    def gz_sends(way, m):
        sends = (b + m <= NZ - 1) if way == 0 else (b - m >= 0)
        comes = (b >= 1) if way == 0 else (b <= NZ - 2)
        return sends, sends & comes

    def gz_round(set_, m, add):
        for piece in range(2):
            for way in range(2):
                sends, comes = gz_sends(way, m)
                if add:

                    @pl.when(comes)
                    def _():
                        gz_add(set_, way, m, piece)

                if m > 0:

                    @pl.when(sends)
                    def _():
                        gz_send(set_, way, m, piece)

    def gy_round(set_, m):
        for piece in range(2):
            for way in range(2):
                order = 1 - piece if way == 0 else piece
                gy_add(set_, way, m, order)
                if m > 0:
                    gy_send(set_, way, m, order)

    def g_round(set_, number):
        if number == 0:
            make_i(set_, 4)
            gy_send(set_, 0, 4, 0)
            gy_send(set_, 1, 4, 1)
            make_j(set_, 3)
            make_j(set_, 1)
            gz_round(set_, 3, False)
            make_i(set_, 3)
            make_i(set_, 5)
            gy_send(set_, 0, 3, 1)
            gy_send(set_, 1, 3, 0)
            make_j(set_, 2)
            for k in (2, 6, 1, 7, 0):
                make_i(set_, k)
            make_j(set_, 0)
        if number == 1:
            gy_add(set_, 0, 3, 0)
            gy_send(set_, 0, 3, 0)
            gy_add(set_, 1, 3, 1)
            gy_send(set_, 1, 3, 1)
            gz_round(set_, 2, True)
        if number == 2:
            gy_round(set_, 2)
            gz_round(set_, 1, True)
        if number == 3:
            gy_round(set_, 1)
        if number == 4:
            gz_round(set_, 0, True)
            gy_round(set_, 0)

    def late_first():
        late_pass(7)
        late_pass(6)

    def late_last():
        y_late(3)
        late_pass(5)

    def inverse_parts():
        for k in range(NY):
            keep(k, inv_s[slot(k)])
        g_round(0, 0)

    total_s, total_t = sum_all(0, total, (late_first, late_last, inverse_parts))
    scale_s = pair_count / total_s
    scale_t = pair_count / total_t

    def slope_of(k):
        near_s = dist_s[slot(k)]
        error = near_s * scale_s - dist_t[slot(k)] * scale_t
        return near_s, error, jnp.clip(error, -1.0, 1.0)

    def second_pass(k):
        near_s, error, slope = slope_of(k)
        dist_t[slot(k)] = slope
        times = 2.0 if 1 <= k <= 3 else 1.0
        return times * fold(slope * near_s), times * fold(slope * (error - 0.5 * slope))

    total = second_pass(0)
    for k in range(1, 5):
        total = add(total, second_pass(k))

    def slopes_first():
        for k in range(NY):
            keep(k, (dist_t[slot(k)] if k < 5 else slope_of(k)[2]) * inv_s[slot(k)])
        g_round(1, 0)
        g_round(0, 1)

    def slopes_next():
        g_round(0, 2)
        g_round(1, 1)

    def slopes_last():
        g_round(0, 3)
        g_round(1, 2)

    curvature, huber = sum_all(1, total, (slopes_first, slopes_next, slopes_last))
    loss_ref[...] = jnp.broadcast_to(huber / pair_count, (8, 128))
    factor = curvature * scale_s * scale_s / pair_count
    g_round(1, 3)
    g_round(0, 4)
    g_round(1, 4)
    grad_ref[:, 0:cut] = scale_s * part_j[1, 0:rows] - factor * part_j[0, 0:rows]
    grad_ref[:, cut:ds] = scale_s * part_i[1, 0:rows] - factor * part_i[0, 0:rows]

    for piece in range(4):
        for k in range(4):
            y_copy(piece, k, k + 1, y_down).wait_send()
        for k in range(3):
            y_copy(piece, (NY - k) % NY, NY - k - 1, y_up).wait_send()
        for cond, src, dst, to, way in (
            (b < 3, 0, 3, z_right, 0), (b > 0, 0, 1, z_left, 1),
            ((b >= 1) & (b < 3), 3, 2, z_right, 0), ((b <= 2) & (b > 0), 1, 2, z_left, 1),
            (b == 2, 2, 1, z_right, 0), (b == 1, 2, 3, z_left, 1),
        ):

            @pl.when(cond)
            def _():
                z_copy(piece, src, dst, to, way).wait_send()

    for set_ in range(2):
        for way in range(2):
            gy_copy(set_, way, 4, way).wait_send()
            for m in (3, 2, 1):
                for piece in range(2):
                    gy_copy(set_, way, m, piece).wait_send()
                sends, _ = gz_sends(way, m)

                @pl.when(sends)
                def _():
                    for piece in range(2):
                        gz_copy(set_, way, m, piece).wait_send()


def shards(teacher, student):
    rows, dt = teacher.shape
    ds = student.shape[1]
    batch_rows = rows * lax.axis_size("blk")
    pair_count = 1.0 * lax.axis_size("group") * batch_rows * (batch_rows - 1)
    cut = ds // 2
    ni, nj = NY * rows, NZ * rows
    bf16 = jnp.bfloat16
    y_parts = (2, 2, 4, 2, rows // 2 * (ds - cut) // 128 + 16, 128)
    z_parts = (2, 2, 3, 2, rows // 2 * cut // 128 + 16, 128)
    vmem, dma = pltpu.VMEM, pltpu.SemaphoreType.DMA
    gradient, loss = pl.pallas_call(
        functools.partial(kernel, pair_count),
        out_shape=(
            jax.ShapeDtypeStruct((rows, ds), F32),
            jax.ShapeDtypeStruct((8, 128), F32),
        ),
        in_specs=[pl.BlockSpec(memory_space=pltpu.HBM)] * 2,
        out_specs=[pl.BlockSpec(memory_space=vmem), pl.BlockSpec(memory_space=vmem)],
        scratch_shapes=[
            vmem((ni, dt), bf16), vmem((ni, ds), bf16), vmem((nj, dt), bf16), vmem((nj, ds), bf16),
            vmem((ni, nj), F32), vmem((ni, nj), F32), vmem((ni, nj), F32),
            vmem((8, nj), F32), vmem((8, nj), F32), vmem((ni, 128), F32), vmem((ni, 128), F32),
            vmem((ni, nj), bf16), vmem((nj, ni), bf16),
            vmem((2, ni, ds - cut), F32), vmem((2, nj, cut), F32),
            vmem(y_parts, bf16), vmem(z_parts, bf16), vmem(y_parts, bf16), vmem(z_parts, bf16),
            vmem((6, NP, 8, 128), F32),
            dma((4,)), dma((4, NY)), dma((4, NY)), dma((4, 2, NZ)), dma((4, NZ)),
            dma((6, NP)), dma((6, NP)),
            dma((2, 2, 4, 2)), dma((2, 2, 4, 2)), dma((2, 2, 3, 2)), dma((2, 2, 3, 2)),
            pltpu.SemaphoreType.REGULAR((3,)),
        ],
        compiler_params=pltpu.CompilerParams(
            collective_id=0, has_side_effects=True, vmem_limit_bytes=62 * 1024 * 1024
        ),
    )(teacher, student)
    return (gradient, loss[0, 0])


def solution(mesh):
    in_specs = (P(("group", "blk"), None), P(("group", "blk"), None))
    out_specs = (P(("group", "blk"), None), P())
    return jax.shard_map(shards, mesh=mesh, in_specs=in_specs, out_specs=out_specs, check_vma=False)
```

```python
import functools
import jax
import jax.numpy as jnp
from jax import lax
from jax.experimental import pallas as pl
from jax.experimental.pallas import tpu as pltpu
from jax.sharding import PartitionSpec as P

MESH = pl.DeviceIdType.MESH
F32 = jnp.float32
NY = 8
NZ = 4
LATE = 12.0
SPAN = 4096.0
NX = 4
NP = 8
NT = (((1,), (1,)), ((), ()))


def fold(values):
    rows, columns = values.shape
    part = jnp.sum(values.reshape(rows // 8, 8, columns), 0)
    total = part[:, 0:128]
    for k in range(1, columns // 128):
        total = total + part[:, k * 128 : (k + 1) * 128]
    return total


def kernel(
    pair_count,
    t_ref, s_ref, grad_ref, loss_ref,
    ti, si, tj, sj,
    dist_t, dist_s, inv_s, norm_t, norm_s, own_t, own_s,
    w_ij, w_ji, part_i, part_j,
    out_y, out_z, in_y, in_z, top_i, top_j,
    sums,
    load, send_y, recv_y, send_z, recv_z,
    send_sum, recv_sum,
    send_gy, recv_gy, send_gz, recv_gz,
    inside,
):
    rows = t_ref.shape[0]
    ds = s_ref.shape[1]
    half = rows // 2
    cut = part_j.shape[2]
    group = lax.axis_index("group")
    blk = lax.axis_index("blk")
    b, c = blk // NY, lax.rem(blk, NY)
    core, x = lax.rem(group, 2), lax.rem(group // 2, NX)
    z = (group // (2 * NX)) * NZ + b
    xc = x * 2 + core

    def device(z, x, core, y):
        return ((z // NZ * NX + x) * 2 + core, lax.rem(z, NZ) * NY + y)

    def y_device(index):
        return device(z, x, core, index)

    def z_device(index):
        return device(index, x, core, c)

    def xc_device(index):
        return device(z, index // 2, lax.rem(index, 2), c)

    stages = ((z_device, z), (xc_device, xc), (y_device, c))

    y_right, y_left = y_device(lax.rem(c + 1, NY)), y_device(lax.rem(c + NY - 1, NY))
    z_right, z_left = z_device(lax.rem(z + 1, NP)), z_device(lax.rem(z + NP - 1, NP))
    near = (
        y_right, y_left, z_right, z_left,
        device(z, lax.rem(x + 1, NX), core, c), device(z, lax.rem(x + NX - 1, NX), core, c),
        device(z, x, 1 - core, c),
    )

    barrier = pltpu.get_barrier_semaphore()
    for other in near:
        pl.semaphore_signal(barrier, inc=1, device_id=other, device_id_type=MESH)

    def slot(k):
        return pl.ds(k * rows, rows)

    loads = [
        pltpu.make_async_copy(src, dst.at[slot(0)], load.at[n])
        for n, (src, dst) in enumerate(((s_ref, si), (s_ref, sj), (t_ref, ti), (t_ref, tj)))
    ]
    for copy in loads:
        copy.start()
    for copy in loads:
        copy.wait()
    pl.semaphore_wait(barrier, len(near))

    def round_signal(r):
        for other in near:
            pl.semaphore_signal(inside.at[r], inc=1, device_id=other, device_id_type=MESH)

    def round_wait(r):
        pl.semaphore_wait(inside.at[r], len(near))

    y_up = y_device(lax.rem(c + jnp.where(core == 0, 1, NY - 1), NY))
    y_down = y_device(lax.rem(c + jnp.where(core == 0, NY - 1, 1), NY))

    def piece_of(refs, k, piece):
        return refs[piece // 2].at[pl.ds(k * rows + (piece % 2) * half, half)]

    def y_copy(piece, src, dst, to):
        return pltpu.make_async_remote_copy(
            src_ref=piece_of((si, ti), src, piece), dst_ref=piece_of((si, ti), dst, piece),
            send_sem=send_y.at[piece, dst], recv_sem=recv_y.at[piece, dst],
            device_id=to, device_id_type=MESH,
        )

    def place(k, b):
        last = jnp.where(b == 0, 3, jnp.where(b == 3, 1, 2))
        return jnp.where(last == k, 3, last if k == 3 else k)

    def z_piece(k, b, piece):
        start = pl.multiple_of(place(k, b) * rows + (piece % 2) * half, half)
        return (sj, tj)[piece // 2].at[pl.ds(start, half)]

    def z_copy(piece, src, dst, to, way):
        return pltpu.make_async_remote_copy(
            src_ref=z_piece(src, b, piece), dst_ref=z_piece(dst, b + (1, -1)[way], piece),
            send_sem=send_z.at[piece, way, dst], recv_sem=recv_z.at[piece, dst],
            device_id=to, device_id_type=MESH,
        )

    def z_wait(piece, dst):
        pltpu.make_async_remote_copy(
            src_ref=z_piece(0, b, piece), dst_ref=z_piece(dst, b, piece),
            send_sem=send_z.at[piece, 0, dst], recv_sem=recv_z.at[piece, dst],
            device_id=z_right, device_id_type=MESH,
        ).wait_recv()

    def y_early(k, piece):
        if k > 0:
            y_copy(piece, k - 1, k, y_down).wait_recv()
        if k < 4:
            y_copy(piece, k, k + 1, y_down).start()

    def y_late(k, piece):
        if k > 0:
            y_copy(piece, (NY + 1 - k) % NY, NY - k, y_up).wait_recv()
        if k < 3:
            y_copy(piece, (NY - k) % NY, NY - k - 1, y_up).start()

    def z_step(k, piece):
        if k == 0:

            @pl.when(b < 3)
            def _():
                z_copy(piece, 0, 3, z_right, 0).start()

            @pl.when(b > 0)
            def _():
                z_copy(piece, 0, 1, z_left, 1).start()

        if k == 1:

            @pl.when(b >= 1)
            def _():
                z_wait(piece, 3)

            @pl.when((b >= 1) & (b < 3))
            def _():
                z_copy(piece, 3, 2, z_right, 0).start()

            @pl.when(b <= 2)
            def _():
                z_wait(piece, 1)

            @pl.when((b <= 2) & (b > 0))
            def _():
                z_copy(piece, 1, 2, z_left, 1).start()

        if k == 2:
            z_wait(piece, 2)

            @pl.when(b == 2)
            def _():
                z_copy(piece, 2, 1, z_right, 0).start()

            @pl.when(b == 1)
            def _():
                z_copy(piece, 2, 3, z_left, 1).start()

        if k == 3:

            @pl.when(b == 0)
            def _():
                z_wait(piece, 3)

            @pl.when(b == 3)
            def _():
                z_wait(piece, 1)

    def squares_of(values):
        wide = values.astype(F32)
        return jnp.sum(wide * wide, 1, keepdims=True)

    def norms_j(k):
        for ref, norm in ((tj, norm_t), (sj, norm_s)):
            squares = squares_of(ref[slot(k)])
            norm[:, k * rows : (k + 1) * rows] = jnp.transpose(jnp.broadcast_to(squares, (rows, 128)))[0:8]

    def norms_i(at):
        for ref, norm in ((ti, own_t), (si, own_s)):
            own = ref[at]
            norm[at] = jnp.broadcast_to(squares_of(own), (own.shape[0], 128))

    def distance(ref, other, own_norm, norm, at, lo, hi):
        products = lax.dot_general(ref[at], other[lo:hi], NT, preferred_element_type=F32)
        spread = own_norm[at][:, 0:1] + norm[0:1, lo:hi] - 2.0 * products
        return jnp.sqrt(jnp.maximum(spread, 0.0) + 1.0)

    def distances(at, lo, hi, diagonal):
        near_t = distance(ti, tj, own_t, norm_t, at, lo, hi)
        near_s = distance(si, sj, own_s, norm_s, at, lo, hi)
        inverse = 1.0 / near_s
        if diagonal:
            row = lax.broadcasted_iota(jnp.int32, near_s.shape, 0)
            off = row != lax.broadcasted_iota(jnp.int32, near_s.shape, 1)
            near_t = jnp.where(off, near_t, 0.0)
            near_s = jnp.where(off, near_s, 0.0)
            inverse = jnp.where(off, inverse, 0.0)
        dist_t[at, lo:hi] = near_t
        dist_s[at, lo:hi] = near_s
        inv_s[at, lo:hi] = inverse
        return near_s, near_t

    def first_pass(k):
        times = 2.0 if 1 <= k <= 3 else 1.0
        return [times * fold(near) for near in distances(slot(k), 0, 3 * rows, k == 0)]

    def add(one, two):
        return [a + b for a, b in zip(one, two)]

    total = [jnp.zeros((8, 128), F32)] * 2

    def pass_now(k):
        total[:] = add(total, first_pass(k))

    def round_next(r):
        round_wait(r)
        if r < 2:
            round_signal(r + 1)

    steps = [(0.0, round_signal, (0,))]
    for p in range(4):
        steps += [(0.1 * p - 1.0, y_early, (0, p)), (0.1 * p - 0.95, z_step, (0, p))]
        steps += [(2.6 + 4.6 * (k - 1) + 1.15 * (p + 1), y_early, (k, p)) for k in range(1, 5)]
        steps += [(2.6 + 9.2 * (k - 1) + 2.3 * (p + 1), z_step, (k, p)) for k in range(1, 3)]
        steps += [(90.0 + p, z_step, (3, p))]
        steps += [(LATE + 0.01 * p, y_late, (0, p))]
        steps += [(LATE + 2.6 + 4.6 * (k - 1) + 1.15 * (p + 1), y_late, (k, p)) for k in range(1, 3)]
    steps += [(2.6 + 4.6 * k + 0.2, norms_i, (slot(k),)) for k in range(5)]
    steps += [(0.1, norms_j, (0,)), (21.05, norms_j, (1,)), (21.1, norms_j, (2,))]
    steps += [(21.2 + 1.2 * k, pass_now, (k,)) for k in range(4)] + [(29.0, pass_now, (4,))]
    steps += [(7.5 + 4.0 * r, round_next, (r,)) for r in range(3)]
    for _, step, args in sorted(steps, key=lambda one: one[0]):
        step(*args)
    norms_j(3)

    def last_pass(start, count, times):
        near = distances(pl.ds(start * rows, count * rows), 3 * rows, 4 * rows, False)
        return [times * fold(one) for one in near]

    total = add(total, last_pass(0, 1, 1.0))
    total = add(total, last_pass(1, 3, 2.0))
    total = add(total, last_pass(4, 1, 1.0))

    def sum_all(which, pair, meanwhile):
        one, two = (jnp.sum(tile, 0, keepdims=True) for tile in pair)
        first = lax.broadcasted_iota(jnp.int32, (8, 128), 0) == 0
        tile = jnp.where(first, one, two)
        for stage, (where, me) in enumerate(stages):
            at = which * 3 + stage
            sums[at, me] = tile

            def copy(j, row):
                return pltpu.make_async_remote_copy(
                    src_ref=sums.at[at, row], dst_ref=sums.at[at, row],
                    send_sem=send_sum.at[at, j], recv_sem=recv_sum.at[at, row],
                    device_id=where(lax.rem(me + j, NP)), device_id_type=MESH,
                )

            for j in (4, 3, 5, 2, 6, 1, 7):
                copy(j, me).start()
            meanwhile[stage]()
            for j in range(1, NP):
                copy(j, lax.rem(me + j, NP)).wait_recv()
            tile = sums[at, 0]
            for j in range(1, NP):
                tile = tile + sums[at, j]
            for j in range(1, NP):
                copy(j, me).wait_send()
        wide = jnp.sum(tile, 1, keepdims=True)
        return wide[0:1], wide[1:2]

    def late_pass(k):
        norms_i(slot(k))
        distances(slot(k), 0, NZ * rows, False)

    def keep(set_, k):
        weight = inv_s[slot(k)]
        if set_ == 1:
            weight = weight * (dist_t[slot(k)] if k < 5 else slope_of(k)[2])
        w_ij[slot(k)] = weight.astype(jnp.bfloat16)
        w_ji[:, k * rows : (k + 1) * rows] = jnp.transpose(weight).astype(jnp.bfloat16)

    def make_i(set_, k):
        weight = w_ij[slot(k)]
        count = jnp.sum(weight.astype(F32), 1, keepdims=True)
        part = si[slot(k), cut:ds].astype(F32) * count - jnp.dot(
            weight, sj[:, cut:ds], preferred_element_type=F32
        )
        part_i[set_, slot(k)] = part
        for piece in range(2):
            top_i[set_, k, piece] = bound(part[piece * half : (piece + 1) * half])

    def make_j(set_, k):
        at = pl.ds(pl.multiple_of(place(k, b) * rows, rows), rows)
        weight = w_ji[at]
        count = jnp.sum(weight.astype(F32), 1, keepdims=True)
        part = sj[at, 0:cut].astype(F32) * count - jnp.dot(
            weight, si[:, 0:cut], preferred_element_type=F32
        )
        part_j[set_, slot(k)] = part
        for piece in range(2):
            top_j[set_, k, piece] = bound(part[piece * half : (piece + 1) * half])

    def g_at(count, way, m, piece):
        return pl.ds((m if way == 0 else (count - m) % count) * rows + piece * half, half)

    def bound(values):
        largest = jnp.max(jnp.max(jnp.abs(values), 1, keepdims=True), 0, keepdims=True)
        return jnp.broadcast_to(jnp.maximum(largest, 1e-30), (8, 128))

    def code(out, values, top):
        scale = top[0:1].astype(jnp.bfloat16)
        ratio = SPAN / scale.astype(F32)
        width = values.shape[1]
        for n in range(width // 128):
            near = values[:, n * 128 : (n + 1) * 128] * ratio
            square = near * near
            coded = near * jnp.abs(near) * square * (square * square)
            out[n * half : (n + 1) * half] = coded.astype(jnp.bfloat16)
        out[half * (width // 128) :] = jnp.broadcast_to(scale, (16, 128))

    def decode(ref, width):
        scale = ref[half * (width // 128) :].astype(F32)[0:8]
        blocks = []
        for n in range(width // 128):
            coded = ref[n * half : (n + 1) * half].astype(F32)
            root = jnp.sqrt(jnp.sqrt(jnp.sqrt(jnp.abs(coded)))) * (scale[0:1] * (1.0 / SPAN))
            blocks.append(jnp.where(coded < 0.0, -root, root))
        return jnp.concatenate(blocks, 1), scale

    def gy_copy(set_, way, m, piece):
        return pltpu.make_async_remote_copy(
            src_ref=out_y.at[set_, way, m - 1, piece], dst_ref=in_y.at[set_, way, m - 1, piece],
            send_sem=send_gy.at[set_, way, m - 1, piece], recv_sem=recv_gy.at[set_, way, m - 1, piece],
            device_id=(y_up, y_down)[way], device_id_type=MESH,
        )

    def gy_send(set_, way, m, piece):
        k = m if way == 0 else (NY - m) % NY
        code(out_y.at[set_, way, m - 1, piece], part_i[set_, g_at(NY, way, m, piece)], top_i[set_, k, piece])
        gy_copy(set_, way, m, piece).start()

    def gy_add(set_, way, m, piece):
        gy_copy(set_, way, m + 1, piece).wait_recv()
        at = g_at(NY, way, m, piece)
        k = m if way == 0 else (NY - m) % NY
        values, scale = decode(in_y.at[set_, way, m, piece], ds - cut)
        part_i[set_, at] = part_i[set_, at] + values
        top_i[set_, k, piece] = top_i[set_, k, piece] + scale

    def gz_copy(set_, way, m, piece):
        return pltpu.make_async_remote_copy(
            src_ref=out_z.at[set_, way, m - 1, piece], dst_ref=in_z.at[set_, way, m - 1, piece],
            send_sem=send_gz.at[set_, way, m - 1, piece], recv_sem=recv_gz.at[set_, way, m - 1, piece],
            device_id=(z_right, z_left)[way], device_id_type=MESH,
        )

    def gz_send(set_, way, m, piece):
        k = m if way == 0 else (NZ - m) % NZ
        code(out_z.at[set_, way, m - 1, piece], part_j[set_, g_at(NZ, way, m, piece)], top_j[set_, k, piece])
        gz_copy(set_, way, m, piece).start()

    def gz_add(set_, way, m, piece):
        gz_copy(set_, way, m + 1, piece).wait_recv()
        at = g_at(NZ, way, m, piece)
        k = m if way == 0 else (NZ - m) % NZ
        values, scale = decode(in_z.at[set_, way, m, piece], cut)
        part_j[set_, at] = part_j[set_, at] + values
        top_j[set_, k, piece] = top_j[set_, k, piece] + scale

    def gz_sends(way, m):
        sends = (b + m <= NZ - 1) if way == 0 else (b - m >= 0)
        comes = (b >= 1) if way == 0 else (b <= NZ - 2)
        return sends, sends & comes

    def gz_round(set_, m, add):
        for piece in range(2):
            for way in range(2):
                sends, comes = gz_sends(way, m)
                if add:

                    @pl.when(comes)
                    def _():
                        gz_add(set_, way, m, piece)

                if m > 0:

                    @pl.when(sends)
                    def _():
                        gz_send(set_, way, m, piece)

    def gy_round(set_, m):
        for piece in range(2):
            for way in range(2):
                order = 1 - piece if way == 0 else piece
                gy_add(set_, way, m, order)
                if m > 0:
                    gy_send(set_, way, m, order)

    def g_round(set_, number):
        if number == 0:
            keep(set_, 4)
            make_i(set_, 4)
            gy_send(set_, 0, 4, 0)
            gy_send(set_, 1, 4, 1)
            for k in (3, 5):
                keep(set_, k)
                make_i(set_, k)
            gy_send(set_, 0, 3, 1)
            gy_send(set_, 1, 3, 0)
            for k in (2, 6, 1, 7, 0):
                keep(set_, k)
            make_j(set_, 3)
            make_j(set_, 1)
            gz_round(set_, 3, False)
            make_j(set_, 2)
            for k in (2, 6, 1, 7, 0):
                make_i(set_, k)
            make_j(set_, 0)
        if number == 1:
            gy_add(set_, 0, 3, 0)
            gy_send(set_, 0, 3, 0)
            gy_add(set_, 1, 3, 1)
            gy_send(set_, 1, 3, 1)
            gz_round(set_, 2, True)
        if number == 2:
            gy_round(set_, 2)
            gz_round(set_, 1, True)
        if number == 3:
            gy_round(set_, 1)
        if number == 4:
            gz_round(set_, 0, True)
            gy_round(set_, 0)

    def late_first():
        late_pass(7)
        late_pass(6)

    def late_last():
        for p in range(4):
            y_late(3, p)
        late_pass(5)

    def inverse_parts():
        g_round(0, 0)

    total_s, total_t = sum_all(0, total, (late_first, late_last, inverse_parts))
    scale_s = pair_count / total_s
    scale_t = pair_count / total_t

    def slope_of(k):
        near_s = dist_s[slot(k)]
        error = near_s * scale_s - dist_t[slot(k)] * scale_t
        return near_s, error, jnp.clip(error, -1.0, 1.0)

    def second_pass(k):
        near_s, error, slope = slope_of(k)
        dist_t[slot(k)] = slope
        times = 2.0 if 1 <= k <= 3 else 1.0
        return times * fold(slope * near_s), times * fold(slope * (error - 0.5 * slope))

    total = second_pass(0)
    for k in range(1, 5):
        total = add(total, second_pass(k))

    def slopes_first():
        g_round(1, 0)
        g_round(0, 1)
        g_round(1, 1)

    def slopes_next():
        g_round(0, 2)
        g_round(1, 2)

    def slopes_last():
        g_round(0, 3)
        g_round(1, 3)

    curvature, huber = sum_all(1, total, (slopes_first, slopes_next, slopes_last))
    loss_ref[...] = jnp.broadcast_to(huber / pair_count, (8, 128))
    factor = curvature * scale_s * scale_s / pair_count
    g_round(0, 4)
    g_round(1, 4)
    grad_ref[:, 0:cut] = scale_s * part_j[1, 0:rows] - factor * part_j[0, 0:rows]
    grad_ref[:, cut:ds] = scale_s * part_i[1, 0:rows] - factor * part_i[0, 0:rows]

    for piece in range(4):
        for k in range(4):
            y_copy(piece, k, k + 1, y_down).wait_send()
        for k in range(3):
            y_copy(piece, (NY - k) % NY, NY - k - 1, y_up).wait_send()
        for cond, src, dst, to, way in (
            (b < 3, 0, 3, z_right, 0), (b > 0, 0, 1, z_left, 1),
            ((b >= 1) & (b < 3), 3, 2, z_right, 0), ((b <= 2) & (b > 0), 1, 2, z_left, 1),
            (b == 2, 2, 1, z_right, 0), (b == 1, 2, 3, z_left, 1),
        ):

            @pl.when(cond)
            def _():
                z_copy(piece, src, dst, to, way).wait_send()

    for set_ in range(2):
        for way in range(2):
            gy_copy(set_, way, 4, way).wait_send()
            for m in (3, 2, 1):
                for piece in range(2):
                    gy_copy(set_, way, m, piece).wait_send()
                sends, _ = gz_sends(way, m)

                @pl.when(sends)
                def _():
                    for piece in range(2):
                        gz_copy(set_, way, m, piece).wait_send()


def shards(teacher, student):
    rows, dt = teacher.shape
    ds = student.shape[1]
    batch_rows = rows * lax.axis_size("blk")
    pair_count = 1.0 * lax.axis_size("group") * batch_rows * (batch_rows - 1)
    cut = ds // 2
    ni, nj = NY * rows, NZ * rows
    bf16 = jnp.bfloat16
    y_parts = (2, 2, 4, 2, rows // 2 * (ds - cut) // 128 + 16, 128)
    z_parts = (2, 2, 3, 2, rows // 2 * cut // 128 + 16, 128)
    vmem, dma = pltpu.VMEM, pltpu.SemaphoreType.DMA
    gradient, loss = pl.pallas_call(
        functools.partial(kernel, pair_count),
        out_shape=(
            jax.ShapeDtypeStruct((rows, ds), F32),
            jax.ShapeDtypeStruct((8, 128), F32),
        ),
        in_specs=[pl.BlockSpec(memory_space=pltpu.HBM)] * 2,
        out_specs=[pl.BlockSpec(memory_space=vmem), pl.BlockSpec(memory_space=vmem)],
        scratch_shapes=[
            vmem((ni, dt), bf16), vmem((ni, ds), bf16), vmem((nj, dt), bf16), vmem((nj, ds), bf16),
            vmem((ni, nj), F32), vmem((ni, nj), F32), vmem((ni, nj), F32),
            vmem((8, nj), F32), vmem((8, nj), F32), vmem((ni, 128), F32), vmem((ni, 128), F32),
            vmem((ni, nj), bf16), vmem((nj, ni), bf16),
            vmem((2, ni, ds - cut), F32), vmem((2, nj, cut), F32),
            vmem(y_parts, bf16), vmem(z_parts, bf16), vmem(y_parts, bf16), vmem(z_parts, bf16),
            vmem((2, NY, 2, 8, 128), F32), vmem((2, NZ, 2, 8, 128), F32),
            vmem((6, NP, 8, 128), F32),
            dma((4,)), dma((4, NY)), dma((4, NY)), dma((4, 2, NZ)), dma((4, NZ)),
            dma((6, NP)), dma((6, NP)),
            dma((2, 2, 4, 2)), dma((2, 2, 4, 2)), dma((2, 2, 3, 2)), dma((2, 2, 3, 2)),
            pltpu.SemaphoreType.REGULAR((3,)),
        ],
        compiler_params=pltpu.CompilerParams(
            collective_id=0, has_side_effects=True, vmem_limit_bytes=52 * 1024 * 1024
        ),
    )(teacher, student)
    return (gradient, loss[0, 0])


def solution(mesh):
    in_specs = (P(("group", "blk"), None), P(("group", "blk"), None))
    out_specs = (P(("group", "blk"), None), P())
    return jax.shard_map(shards, mesh=mesh, in_specs=in_specs, out_specs=out_specs, check_vma=False)
```

```python
import functools
import jax
import jax.numpy as jnp
from jax import lax
from jax.experimental import pallas as pl
from jax.experimental.pallas import tpu as pltpu
from jax.sharding import PartitionSpec as P

MESH = pl.DeviceIdType.MESH
F32 = jnp.float32
NY = 8
NZ = 4
LATE = 12.0
SPAN = 4096.0
NX = 4
NP = 8
NT = (((1,), (1,)), ((), ()))


def fold(values):
    rows, columns = values.shape
    part = jnp.sum(values.reshape(rows // 8, 8, columns), 0)
    total = part[:, 0:128]
    for k in range(1, columns // 128):
        total = total + part[:, k * 128 : (k + 1) * 128]
    return total


def kernel(
    pair_count,
    t_ref, s_ref, grad_ref, loss_ref,
    ti, si, tj, sj,
    dist_t, dist_s, inv_s, norm_t, norm_s, own_t, own_s,
    w_ij, w_ji, part_i, part_j,
    out_y, out_z, in_y, in_z, top_i, top_j,
    sums,
    load, send_y, recv_y, send_z, recv_z,
    send_sum, recv_sum,
    send_gy, recv_gy, send_gz, recv_gz,
    inside,
):
    rows = t_ref.shape[0]
    ds = s_ref.shape[1]
    half = rows // 2
    cut = part_j.shape[2]
    group = lax.axis_index("group")
    blk = lax.axis_index("blk")
    b, c = blk // NY, lax.rem(blk, NY)
    core, x = lax.rem(group, 2), lax.rem(group // 2, NX)
    z = (group // (2 * NX)) * NZ + b
    xc = x * 2 + core

    def device(z, x, core, y):
        return ((z // NZ * NX + x) * 2 + core, lax.rem(z, NZ) * NY + y)

    def y_device(index):
        return device(z, x, core, index)

    def z_device(index):
        return device(index, x, core, c)

    def xc_device(index):
        return device(z, index // 2, lax.rem(index, 2), c)

    stages = ((z_device, z), (xc_device, xc), (y_device, c))

    y_right, y_left = y_device(lax.rem(c + 1, NY)), y_device(lax.rem(c + NY - 1, NY))
    z_right, z_left = z_device(lax.rem(z + 1, NP)), z_device(lax.rem(z + NP - 1, NP))
    near = (
        y_right, y_left, z_right, z_left,
        device(z, lax.rem(x + 1, NX), core, c), device(z, lax.rem(x + NX - 1, NX), core, c),
        device(z, x, 1 - core, c),
    )

    barrier = pltpu.get_barrier_semaphore()
    for other in near:
        pl.semaphore_signal(barrier, inc=1, device_id=other, device_id_type=MESH)

    def slot(k):
        return pl.ds(k * rows, rows)

    loads = [
        pltpu.make_async_copy(src, dst.at[slot(0)], load.at[n])
        for n, (src, dst) in enumerate(((s_ref, si), (s_ref, sj), (t_ref, ti), (t_ref, tj)))
    ]
    for copy in loads:
        copy.start()
    pl.semaphore_wait(barrier, len(near))

    def round_signal(r):
        for other in near:
            pl.semaphore_signal(inside.at[r], inc=1, device_id=other, device_id_type=MESH)

    def round_wait(r):
        pl.semaphore_wait(inside.at[r], len(near))

    y_up = y_device(lax.rem(c + jnp.where(core == 0, 1, NY - 1), NY))
    y_down = y_device(lax.rem(c + jnp.where(core == 0, NY - 1, 1), NY))

    def piece_of(refs, k, piece):
        return refs[piece // 2].at[pl.ds(k * rows + (piece % 2) * half, half)]

    def y_copy(piece, src, dst, to):
        return pltpu.make_async_remote_copy(
            src_ref=piece_of((s_ref, t_ref) if src == 0 else (si, ti), src, piece),
            dst_ref=piece_of((si, ti), dst, piece),
            send_sem=send_y.at[piece, dst], recv_sem=recv_y.at[piece, dst],
            device_id=to, device_id_type=MESH,
        )

    def place(k, b):
        last = jnp.where(b == 0, 3, jnp.where(b == 3, 1, 2))
        return jnp.where(last == k, 3, last if k == 3 else k)

    def z_piece(k, b, piece):
        start = pl.multiple_of(place(k, b) * rows + (piece % 2) * half, half)
        return (sj, tj)[piece // 2].at[pl.ds(start, half)]

    def z_copy(piece, src, dst, to, way):
        return pltpu.make_async_remote_copy(
            src_ref=piece_of((s_ref, t_ref), 0, piece) if src == 0 else z_piece(src, b, piece),
            dst_ref=z_piece(dst, b + (1, -1)[way], piece),
            send_sem=send_z.at[piece, way, dst], recv_sem=recv_z.at[piece, dst],
            device_id=to, device_id_type=MESH,
        )

    def z_wait(piece, dst):
        pltpu.make_async_remote_copy(
            src_ref=z_piece(0, b, piece), dst_ref=z_piece(dst, b, piece),
            send_sem=send_z.at[piece, 0, dst], recv_sem=recv_z.at[piece, dst],
            device_id=z_right, device_id_type=MESH,
        ).wait_recv()

    def y_early(k, piece):
        if k > 0:
            y_copy(piece, k - 1, k, y_down).wait_recv()
        if k < 4:
            y_copy(piece, k, k + 1, y_down).start()

    def y_late(k, piece):
        if k > 0:
            y_copy(piece, (NY + 1 - k) % NY, NY - k, y_up).wait_recv()
        if k < 3:
            y_copy(piece, (NY - k) % NY, NY - k - 1, y_up).start()

    def z_step(k, piece):
        if k == 0:

            @pl.when(b < 3)
            def _():
                z_copy(piece, 0, 3, z_right, 0).start()

            @pl.when(b > 0)
            def _():
                z_copy(piece, 0, 1, z_left, 1).start()

        if k == 1:

            @pl.when(b >= 1)
            def _():
                z_wait(piece, 3)

            @pl.when((b >= 1) & (b < 3))
            def _():
                z_copy(piece, 3, 2, z_right, 0).start()

            @pl.when(b <= 2)
            def _():
                z_wait(piece, 1)

            @pl.when((b <= 2) & (b > 0))
            def _():
                z_copy(piece, 1, 2, z_left, 1).start()

        if k == 2:
            z_wait(piece, 2)

            @pl.when(b == 2)
            def _():
                z_copy(piece, 2, 1, z_right, 0).start()

            @pl.when(b == 1)
            def _():
                z_copy(piece, 2, 3, z_left, 1).start()

        if k == 3:

            @pl.when(b == 0)
            def _():
                z_wait(piece, 3)

            @pl.when(b == 3)
            def _():
                z_wait(piece, 1)

    def squares_of(values):
        wide = values.astype(F32)
        return jnp.sum(wide * wide, 1, keepdims=True)

    def norms_j(k):
        for ref, norm in ((tj, norm_t), (sj, norm_s)):
            squares = squares_of(ref[slot(k)])
            norm[:, k * rows : (k + 1) * rows] = jnp.transpose(jnp.broadcast_to(squares, (rows, 128)))[0:8]

    def norms_i(at):
        for ref, norm in ((ti, own_t), (si, own_s)):
            own = ref[at]
            norm[at] = jnp.broadcast_to(squares_of(own), (own.shape[0], 128))

    def distance(ref, other, own_norm, norm, at, lo, hi):
        products = lax.dot_general(ref[at], other[lo:hi], NT, preferred_element_type=F32)
        spread = own_norm[at][:, 0:1] + norm[0:1, lo:hi] - 2.0 * products
        return jnp.sqrt(jnp.maximum(spread, 0.0) + 1.0)

    def distances(at, lo, hi, diagonal):
        near_t = distance(ti, tj, own_t, norm_t, at, lo, hi)
        near_s = distance(si, sj, own_s, norm_s, at, lo, hi)
        inverse = 1.0 / near_s
        if diagonal:
            row = lax.broadcasted_iota(jnp.int32, near_s.shape, 0)
            off = row != lax.broadcasted_iota(jnp.int32, near_s.shape, 1)
            near_t = jnp.where(off, near_t, 0.0)
            near_s = jnp.where(off, near_s, 0.0)
            inverse = jnp.where(off, inverse, 0.0)
        dist_t[at, lo:hi] = near_t
        dist_s[at, lo:hi] = near_s
        inv_s[at, lo:hi] = inverse
        return near_s, near_t

    def first_pass(k):
        times = 2.0 if 1 <= k <= 3 else 1.0
        return [times * fold(near) for near in distances(slot(k), 0, 3 * rows, k == 0)]

    def add(one, two):
        return [a + b for a, b in zip(one, two)]

    total = [jnp.zeros((8, 128), F32)] * 2

    def pass_now(k):
        total[:] = add(total, first_pass(k))

    def round_next(r):
        round_wait(r)
        if r < 2:
            round_signal(r + 1)

    def loaded():
        for copy in loads:
            copy.wait()

    steps = [(0.0, round_signal, (0,)), (0.05, loaded, ())]
    for p in range(4):
        steps += [(0.1 * p - 1.0, y_early, (0, p)), (0.1 * p - 0.95, z_step, (0, p))]
        steps += [(2.6 + 4.6 * (k - 1) + 1.15 * (p + 1), y_early, (k, p)) for k in range(1, 5)]
        steps += [(2.6 + 9.2 * (k - 1) + 2.3 * (p + 1), z_step, (k, p)) for k in range(1, 3)]
        steps += [(90.0 + p, z_step, (3, p))]
        steps += [(LATE + 0.01 * p, y_late, (0, p))]
        steps += [(LATE + 2.6 + 4.6 * (k - 1) + 1.15 * (p + 1), y_late, (k, p)) for k in range(1, 3)]
    steps += [(2.6 + 4.6 * k + 0.2, norms_i, (slot(k),)) for k in range(5)]
    steps += [(0.1, norms_j, (0,)), (21.05, norms_j, (1,)), (21.1, norms_j, (2,))]
    steps += [(21.2 + 1.2 * k, pass_now, (k,)) for k in range(4)] + [(29.0, pass_now, (4,))]
    steps += [(7.5 + 4.0 * r, round_next, (r,)) for r in range(3)]
    for _, step, args in sorted(steps, key=lambda one: one[0]):
        step(*args)
    norms_j(3)

    def last_pass(start, count, times):
        near = distances(pl.ds(start * rows, count * rows), 3 * rows, 4 * rows, False)
        return [times * fold(one) for one in near]

    total = add(total, last_pass(0, 1, 1.0))
    total = add(total, last_pass(1, 3, 2.0))
    total = add(total, last_pass(4, 1, 1.0))

    def sum_all(which, pair, meanwhile):
        one, two = (jnp.sum(tile, 0, keepdims=True) for tile in pair)
        first = lax.broadcasted_iota(jnp.int32, (8, 128), 0) == 0
        tile = jnp.where(first, one, two)
        for stage, (where, me) in enumerate(stages):
            at = which * 3 + stage
            sums[at, me] = tile

            def copy(j, row):
                return pltpu.make_async_remote_copy(
                    src_ref=sums.at[at, row], dst_ref=sums.at[at, row],
                    send_sem=send_sum.at[at, j], recv_sem=recv_sum.at[at, row],
                    device_id=where(lax.rem(me + j, NP)), device_id_type=MESH,
                )

            for j in (4, 3, 5, 2, 6, 1, 7):
                copy(j, me).start()
            meanwhile[stage]()
            for j in range(1, NP):
                copy(j, lax.rem(me + j, NP)).wait_recv()
            tile = sums[at, 0]
            for j in range(1, NP):
                tile = tile + sums[at, j]
            for j in range(1, NP):
                copy(j, me).wait_send()
        wide = jnp.sum(tile, 1, keepdims=True)
        return wide[0:1], wide[1:2]

    def late_pass(k):
        norms_i(slot(k))
        distances(slot(k), 0, NZ * rows, False)

    def keep(set_, k):
        weight = inv_s[slot(k)]
        if set_ == 1:
            weight = weight * (dist_t[slot(k)] if k < 5 else slope_of(k)[2])
        w_ij[slot(k)] = weight.astype(jnp.bfloat16)
        w_ji[:, k * rows : (k + 1) * rows] = jnp.transpose(weight).astype(jnp.bfloat16)

    def make_i(set_, k):
        weight = w_ij[slot(k)]
        count = jnp.sum(weight.astype(F32), 1, keepdims=True)
        part = si[slot(k), cut:ds].astype(F32) * count - jnp.dot(
            weight, sj[:, cut:ds], preferred_element_type=F32
        )
        part_i[set_, slot(k)] = part
        for piece in range(2):
            top_i[set_, k, piece] = bound(part[piece * half : (piece + 1) * half])

    def make_j(set_, k):
        at = pl.ds(pl.multiple_of(place(k, b) * rows, rows), rows)
        weight = w_ji[at]
        count = jnp.sum(weight.astype(F32), 1, keepdims=True)
        part = sj[at, 0:cut].astype(F32) * count - jnp.dot(
            weight, si[:, 0:cut], preferred_element_type=F32
        )
        part_j[set_, slot(k)] = part
        for piece in range(2):
            top_j[set_, k, piece] = bound(part[piece * half : (piece + 1) * half])

    def g_at(count, way, m, piece):
        return pl.ds((m if way == 0 else (count - m) % count) * rows + piece * half, half)

    def bound(values):
        largest = jnp.max(jnp.max(jnp.abs(values), 1, keepdims=True), 0, keepdims=True)
        return jnp.broadcast_to(jnp.maximum(largest, 1e-30), (8, 128))

    def code(out, values, top):
        scale = top[0:1].astype(jnp.bfloat16)
        ratio = SPAN / scale.astype(F32)
        width = values.shape[1]
        for n in range(width // 128):
            near = values[:, n * 128 : (n + 1) * 128] * ratio
            square = near * near
            coded = near * jnp.abs(near) * square * (square * square)
            out[n * half : (n + 1) * half] = coded.astype(jnp.bfloat16)
        out[half * (width // 128) :] = jnp.broadcast_to(scale, (16, 128))

    def decode(ref, width):
        scale = ref[half * (width // 128) :].astype(F32)[0:8]
        blocks = []
        for n in range(width // 128):
            coded = ref[n * half : (n + 1) * half].astype(F32)
            root = jnp.sqrt(jnp.sqrt(jnp.sqrt(jnp.abs(coded)))) * (scale[0:1] * (1.0 / SPAN))
            blocks.append(jnp.where(coded < 0.0, -root, root))
        return jnp.concatenate(blocks, 1), scale

    def gy_copy(set_, way, m, piece):
        return pltpu.make_async_remote_copy(
            src_ref=out_y.at[set_, way, m - 1, piece], dst_ref=in_y.at[set_, way, m - 1, piece],
            send_sem=send_gy.at[set_, way, m - 1, piece], recv_sem=recv_gy.at[set_, way, m - 1, piece],
            device_id=(y_up, y_down)[way], device_id_type=MESH,
        )

    def gy_send(set_, way, m, piece):
        k = m if way == 0 else (NY - m) % NY
        code(out_y.at[set_, way, m - 1, piece], part_i[set_, g_at(NY, way, m, piece)], top_i[set_, k, piece])
        gy_copy(set_, way, m, piece).start()

    def gy_add(set_, way, m, piece):
        gy_copy(set_, way, m + 1, piece).wait_recv()
        at = g_at(NY, way, m, piece)
        k = m if way == 0 else (NY - m) % NY
        values, scale = decode(in_y.at[set_, way, m, piece], ds - cut)
        part_i[set_, at] = part_i[set_, at] + values
        top_i[set_, k, piece] = top_i[set_, k, piece] + scale

    def gz_copy(set_, way, m, piece):
        return pltpu.make_async_remote_copy(
            src_ref=out_z.at[set_, way, m - 1, piece], dst_ref=in_z.at[set_, way, m - 1, piece],
            send_sem=send_gz.at[set_, way, m - 1, piece], recv_sem=recv_gz.at[set_, way, m - 1, piece],
            device_id=(z_right, z_left)[way], device_id_type=MESH,
        )

    def gz_send(set_, way, m, piece):
        k = m if way == 0 else (NZ - m) % NZ
        code(out_z.at[set_, way, m - 1, piece], part_j[set_, g_at(NZ, way, m, piece)], top_j[set_, k, piece])
        gz_copy(set_, way, m, piece).start()

    def gz_add(set_, way, m, piece):
        gz_copy(set_, way, m + 1, piece).wait_recv()
        at = g_at(NZ, way, m, piece)
        k = m if way == 0 else (NZ - m) % NZ
        values, scale = decode(in_z.at[set_, way, m, piece], cut)
        part_j[set_, at] = part_j[set_, at] + values
        top_j[set_, k, piece] = top_j[set_, k, piece] + scale

    def gz_sends(way, m):
        sends = (b + m <= NZ - 1) if way == 0 else (b - m >= 0)
        comes = (b >= 1) if way == 0 else (b <= NZ - 2)
        return sends, sends & comes

    def gz_round(set_, m, add):
        for piece in range(2):
            for way in range(2):
                sends, comes = gz_sends(way, m)
                if add:

                    @pl.when(comes)
                    def _():
                        gz_add(set_, way, m, piece)

                if m > 0:

                    @pl.when(sends)
                    def _():
                        gz_send(set_, way, m, piece)

    def gy_round(set_, m):
        for piece in range(2):
            for way in range(2):
                order = 1 - piece if way == 0 else piece
                gy_add(set_, way, m, order)
                if m > 0:
                    gy_send(set_, way, m, order)

    def g_round(set_, number):
        if number == 0:
            keep(set_, 4)
            make_i(set_, 4)
            gy_send(set_, 0, 4, 0)
            gy_send(set_, 1, 4, 1)
            for k in (3, 5):
                keep(set_, k)
                make_i(set_, k)
            gy_send(set_, 0, 3, 1)
            gy_send(set_, 1, 3, 0)
            for k in (2, 6, 1, 7, 0):
                keep(set_, k)
            make_j(set_, 3)
            make_j(set_, 1)
            gz_round(set_, 3, False)
            make_j(set_, 2)
            for k in (2, 6, 1, 7, 0):
                make_i(set_, k)
            make_j(set_, 0)
        if number == 1:
            gy_add(set_, 0, 3, 0)
            gy_send(set_, 0, 3, 0)
            gy_add(set_, 1, 3, 1)
            gy_send(set_, 1, 3, 1)
            gz_round(set_, 2, True)
        if number == 2:
            gy_round(set_, 2)
            gz_round(set_, 1, True)
        if number == 3:
            gy_round(set_, 1)
        if number == 4:
            gz_round(set_, 0, True)
            gy_round(set_, 0)

    def late_first():
        late_pass(7)
        late_pass(6)

    def late_last():
        for p in range(4):
            y_late(3, p)
        late_pass(5)

    def inverse_parts():
        g_round(0, 0)

    total_s, total_t = sum_all(0, total, (late_first, late_last, inverse_parts))
    scale_s = pair_count / total_s
    scale_t = pair_count / total_t

    def slope_of(k):
        near_s = dist_s[slot(k)]
        error = near_s * scale_s - dist_t[slot(k)] * scale_t
        return near_s, error, jnp.clip(error, -1.0, 1.0)

    def second_pass(k):
        times = 2.0 if 1 <= k <= 3 else 1.0
        sums_of = [jnp.zeros((8, 128), F32)] * 2
        for n in range(NZ):
            at = (slot(k), slice(n * 128, (n + 1) * 128))
            near_s = dist_s[at]
            error = near_s * scale_s - dist_t[at] * scale_t
            slope = jnp.clip(error, -1.0, 1.0)
            dist_t[at] = slope
            sums_of = add(sums_of, (fold(slope * near_s), fold(slope * (error - 0.5 * slope))))
        return [times * one for one in sums_of]

    total = second_pass(0)
    for k in range(1, 5):
        total = add(total, second_pass(k))

    def slopes_first():
        g_round(1, 0)
        g_round(0, 1)
        g_round(1, 1)

    def slopes_next():
        g_round(0, 2)
        g_round(1, 2)

    def slopes_last():
        g_round(0, 3)
        g_round(1, 3)

    curvature, huber = sum_all(1, total, (slopes_first, slopes_next, slopes_last))
    loss_ref[...] = jnp.broadcast_to(huber / pair_count, (8, 128))
    factor = curvature * scale_s * scale_s / pair_count
    g_round(0, 4)
    g_round(1, 4)
    grad_ref[:, 0:cut] = scale_s * part_j[1, 0:rows] - factor * part_j[0, 0:rows]
    grad_ref[:, cut:ds] = scale_s * part_i[1, 0:rows] - factor * part_i[0, 0:rows]

    for piece in range(4):
        for k in range(4):
            y_copy(piece, k, k + 1, y_down).wait_send()
        for k in range(3):
            y_copy(piece, (NY - k) % NY, NY - k - 1, y_up).wait_send()
        for cond, src, dst, to, way in (
            (b < 3, 0, 3, z_right, 0), (b > 0, 0, 1, z_left, 1),
            ((b >= 1) & (b < 3), 3, 2, z_right, 0), ((b <= 2) & (b > 0), 1, 2, z_left, 1),
            (b == 2, 2, 1, z_right, 0), (b == 1, 2, 3, z_left, 1),
        ):

            @pl.when(cond)
            def _():
                z_copy(piece, src, dst, to, way).wait_send()

    for set_ in range(2):
        for way in range(2):
            gy_copy(set_, way, 4, way).wait_send()
            for m in (3, 2, 1):
                for piece in range(2):
                    gy_copy(set_, way, m, piece).wait_send()
                sends, _ = gz_sends(way, m)

                @pl.when(sends)
                def _():
                    for piece in range(2):
                        gz_copy(set_, way, m, piece).wait_send()


def shards(teacher, student):
    rows, dt = teacher.shape
    ds = student.shape[1]
    batch_rows = rows * lax.axis_size("blk")
    pair_count = 1.0 * lax.axis_size("group") * batch_rows * (batch_rows - 1)
    cut = ds // 2
    ni, nj = NY * rows, NZ * rows
    bf16 = jnp.bfloat16
    y_parts = (2, 2, 4, 2, rows // 2 * (ds - cut) // 128 + 16, 128)
    z_parts = (2, 2, 3, 2, rows // 2 * cut // 128 + 16, 128)
    vmem, dma = pltpu.VMEM, pltpu.SemaphoreType.DMA
    gradient, loss = pl.pallas_call(
        functools.partial(kernel, pair_count),
        out_shape=(
            jax.ShapeDtypeStruct((rows, ds), F32),
            jax.ShapeDtypeStruct((8, 128), F32),
        ),
        in_specs=[pl.BlockSpec(memory_space=pltpu.HBM)] * 2,
        out_specs=[pl.BlockSpec(memory_space=vmem), pl.BlockSpec(memory_space=vmem)],
        scratch_shapes=[
            vmem((ni, dt), bf16), vmem((ni, ds), bf16), vmem((nj, dt), bf16), vmem((nj, ds), bf16),
            vmem((ni, nj), F32), vmem((ni, nj), F32), vmem((ni, nj), F32),
            vmem((8, nj), F32), vmem((8, nj), F32), vmem((ni, 128), F32), vmem((ni, 128), F32),
            vmem((ni, nj), bf16), vmem((nj, ni), bf16),
            vmem((2, ni, ds - cut), F32), vmem((2, nj, cut), F32),
            vmem(y_parts, bf16), vmem(z_parts, bf16), vmem(y_parts, bf16), vmem(z_parts, bf16),
            vmem((2, NY, 2, 8, 128), F32), vmem((2, NZ, 2, 8, 128), F32),
            vmem((6, NP, 8, 128), F32),
            dma((4,)), dma((4, NY)), dma((4, NY)), dma((4, 2, NZ)), dma((4, NZ)),
            dma((6, NP)), dma((6, NP)),
            dma((2, 2, 4, 2)), dma((2, 2, 4, 2)), dma((2, 2, 3, 2)), dma((2, 2, 3, 2)),
            pltpu.SemaphoreType.REGULAR((3,)),
        ],
        compiler_params=pltpu.CompilerParams(
            collective_id=0, has_side_effects=True, vmem_limit_bytes=52 * 1024 * 1024
        ),
    )(teacher, student)
    return (gradient, loss[0, 0])


def solution(mesh):
    in_specs = (P(("group", "blk"), None), P(("group", "blk"), None))
    out_specs = (P(("group", "blk"), None), P())
    return jax.shard_map(shards, mesh=mesh, in_specs=in_specs, out_specs=out_specs, check_vma=False)
```
